32 devices in a mesh: ctx: 4 (over y, x), exp: 4 (over z), rep: 2 (over core).
Axes of the slice: x: 2, y: 2, z: 4, core: 2. Of those that a mesh axis runs over, the one named last changes fastest.
Arguments:
- tokens: bfloat16 [1024, 7168], P(('rep', 'exp'), 'ctx'), parts along dimension 0, may hold values from -6 to 6
- routes: int32 [1024, 2], P(('rep', 'exp')), parts along dimension 0, may hold values from 0 to 3, all different within a row; in each aligned block of 128 rows (0 to 127, 128 to 255, ...) at most 80 rows name the same one
- event_weights: float32 [1024, 2], P(('rep', 'exp')), parts along dimension 0, may hold values from 0.25 to 2
- cotangent: bfloat16 [512, 7168], P('exp', 'ctx'), may hold values from -0.59765625 to 0.59765625
- w_gate: bfloat16 [4, 7168, 1024], P('exp', 'ctx'), may hold values from -0.0625 to 0.0625
- w_up: bfloat16 [4, 7168, 1024], P('exp', 'ctx'), may hold values from -0.0625 to 0.0625
- w_down: bfloat16 [4, 1024, 7168], P('exp', None, 'ctx'), may hold values from -0.1875 to 0.1875
Outputs:
- mixed: bfloat16 [1024, 7168], P(('rep', 'exp'), 'ctx'), parts along dimension 0
- token_grad: bfloat16 [1024, 7168], P(('rep', 'exp'), 'ctx'), parts along dimension 0
- weight_grad: float32 [1024, 2], P(('rep', 'exp')), parts along dimension 0
The draws below stay inside these ranges and needn't reach their ends.
There are 2 independent parts, one for each index of `rep`. The reference program is written for one: setup_inputs(seed, part) draws one part's arguments, and reference() takes and returns one part's arrays. A program takes and returns all parts, laid end to end along the dimension named above; an argument that names none is the same for every part. Nothing has to cross between parts.
Inputs may be any that keep to these rules, and one draw needn't show every extreme that they name: `routes`: each token names 2 different experts. Among the 128 tokens of one index of exp (aligned blocks of 128 rows) no expert is named more than 80 times, a bound that some block reaches; every expert is named somewhere.
All inputs are finite; a program needn't handle non-finite values.
Results may differ from the reference program's by a relative error of at most 0.03.
Values may be sent and summed in bfloat16 or wider, within the bound.
A program may use at most 64 MiB of HBM per device.

```python
import math
import jax
import jax.numpy as jnp
import numpy as np
from jax import lax

D = 7168
TOP = 2
FH = 1024
TOK_E = 128
EXPERTS = 4
CAP = 80
TOKENS = 512
N_CTX = 4
N_EXP = 4


def level_of(rng, dims, shards, low, largest):
    gain, own = 1.0, jax.random.fold_in(rng, 6)
    for position, shards_of in shards:
        draws = jnp.exp(jax.random.uniform(jax.random.fold_in(own, position), (shards_of,), jnp.float32, low / len(shards), largest / len(shards)))
        gain = gain * jnp.repeat(draws, dims[position] // shards_of).reshape([-1 if axis == position else 1 for axis in range(len(dims))])
    return gain


def deal_out(key, own, number, rows, number_of, top, bound, lean):
    sequence = jax.random.permutation(key, number_of)
    crowded, common = portions_of(number_of, rows * top, bound, lean, True), portions_of(number_of, rows * top, bound, lean, False)
    places = jnp.arange(number_of)

    def named(lengths, rotation):
        used = int((lengths > 0).sum())
        fixed = max(1, used // 4)
        passed = fixed + (places - fixed + rotation * (used - fixed)) % max(1, number_of - fixed)
        return jnp.zeros((number_of,), jnp.int32).at[sequence[jnp.where(places < fixed, places, passed)]].set(jnp.asarray(lengths, jnp.int32))

    lengths = jnp.where(number % 4 == 0, named(crowded, number // 4), named(common, number - number // 4 - 1))
    mixed = jax.random.permutation(jax.random.fold_in(own, 3), number_of)
    donor, taker = mixed[0:number_of // 2 * 2:2], mixed[1:number_of // 2 * 2:2]
    slack = jnp.minimum(lengths[donor] - 1, bound - lengths[taker]) // 2
    slack = jnp.where((donor == sequence[0]) | (taker == sequence[0]) | (lengths[taker] == 0), 0, jnp.maximum(slack, 0))
    passed = jax.random.randint(jax.random.fold_in(own, 4), (number_of // 2,), 0, 1 << 20) % (slack + 1)
    lengths = lengths.at[donor].add(-passed).at[taker].add(passed)
    items = jnp.searchsorted(jnp.cumsum(lengths), jnp.arange(rows * top), side="right").astype(jnp.int32)
    table = items.reshape(top, rows).T
    table = table[jax.random.permutation(jax.random.fold_in(own, 1), rows)]
    rotation = jax.random.randint(jax.random.fold_in(own, 2), (rows, 1), 0, top)
    return jnp.take_along_axis(table, (jnp.arange(top)[None, :] + rotation) % top, axis=1)


def portions_of(count, total, most, skew, full):
    loads = [(1 << 20) // math.isqrt(grade ** skew) + 1 for grade in range(1, count + 1)]
    largest = most if full else min(most, max(-(-total // count), total * loads[0] // sum(loads)))
    least = 1 if total - largest >= count - 1 else 0
    given, spare = [largest] + [least] * (count - 1), total - largest - least * (count - 1)
    while spare > 0:
        candidates = [i for i in range(1, count) if given[i] < largest] or [i for i in range(1, count) if given[i] < most]
        mass, remaining = sum([loads[i] for i in candidates]), spare
        for i in candidates:
            extra = min(most - given[i], max(1, remaining * loads[i] // mass), spare)
            given[i] = given[i] + extra
            spare = spare - extra
    return np.array(given)


def bell_draw(own_key, extent, scale, reach, pieces=(), kind=jnp.bfloat16):
    values = scale * jax.random.normal(own_key, extent, jnp.float32)
    if pieces:
        values = values * level_of(own_key, extent, pieces, -0.22, 0.18)
    return jnp.clip(values, -reach, reach).astype(kind)


def setup_inputs(seed: int = 0, part: int = 0) -> dict:
    splits = jax.random.split(jax.random.key(seed), 8)
    own_keys = jax.random.split(jax.random.fold_in(splits[7], part), 8)
    tokens = bell_draw(own_keys[0], (TOKENS, D), 1.0, 6.0, ((0, 4), (1, 4)))
    routes_keys = jax.random.split(jax.random.fold_in(own_keys[1], 1), TOKENS // TOK_E)
    routes_turns = jax.random.permutation(jax.random.fold_in(own_keys[1], 3), TOKENS // TOK_E)
    routes = jax.vmap(lambda own, number: deal_out(jax.random.fold_in(own_keys[1], 2), own, number, TOK_E, EXPERTS, TOP, CAP, 2))(routes_keys, routes_turns).reshape((TOKENS, TOP))
    event_weights = jnp.clip(jnp.exp(math.log(2.0) - 2.0794415 * jax.random.uniform(own_keys[2], (TOKENS, TOP), jnp.float32) ** level_of(own_keys[2], (TOKENS, TOP), ((0, 4),), -0.2, 0.2)), 0.25, 2.0)
    cotangent = bell_draw(splits[3], (TOKENS, D), 0.1, 0.59765625, ((0, 4), (1, 4)))
    w_gate = bell_draw(splits[4], (EXPERTS, D, FH), D ** -0.5, 0.0625, ((0, 4), (1, 4)))
    w_up = bell_draw(splits[5], (EXPERTS, D, FH), D ** -0.5, 0.0625, ((0, 4), (1, 4)))
    w_down = bell_draw(splits[6], (EXPERTS, FH, D), FH ** -0.5, 0.1875, ((0, 4), (2, 4)))
    return dict(tokens=tokens, routes=routes, event_weights=event_weights, cotangent=cotangent, w_gate=w_gate, w_up=w_up, w_down=w_down)


def slot_places(routes):
    routes_flat = routes.reshape(N_EXP, TOK_E * TOP)
    onehot = (routes_flat[:, :, None] == jnp.arange(EXPERTS, dtype=jnp.int32)[None, None, :]).astype(jnp.int32)
    places = jnp.sum((jnp.cumsum(onehot, axis=1) - onehot) * onehot, axis=2)
    source = jnp.arange(N_EXP, dtype=jnp.int32)[:, None]
    return routes_flat.reshape(-1), (source * CAP + places).reshape(-1).astype(jnp.int32)


def rounded_sum(partial_value):
    narrow = lax.optimization_barrier(partial_value.astype(jnp.bfloat16))
    return jnp.sum(narrow.astype(jnp.float32), axis=0)


def activate(gate_pre, up_pre, back_pre):
    squash = jax.nn.sigmoid(gate_pre)
    hidden_act = (gate_pre * squash * up_pre).astype(jnp.bfloat16)
    grad_gate = (back_pre * up_pre * squash * (1.0 + gate_pre * (1.0 - squash))).astype(jnp.bfloat16)
    grad_up = (back_pre * gate_pre * squash).astype(jnp.bfloat16)
    return hidden_act, grad_gate, grad_up


def reference(tokens, routes, event_weights, cotangent, w_gate, w_up, w_down):
    columns = D // N_CTX
    slot_count = N_EXP * CAP
    expert_ids, slot_rows = slot_places(routes)
    token_rows = jnp.repeat(tokens, TOP, axis=0)
    cot_rows = (event_weights.reshape(-1, 1) * jnp.repeat(cotangent.astype(jnp.float32), TOP, axis=0)).astype(jnp.bfloat16)
    token_buffer = jnp.zeros((EXPERTS, slot_count, D), jnp.bfloat16).at[expert_ids, slot_rows].set(token_rows)
    cot_buffer = jnp.zeros((EXPERTS, slot_count, D), jnp.bfloat16).at[expert_ids, slot_rows].set(cot_rows)

    def one_expert(inputs):
        expert_in, expert_cot, gate_mat, up_mat, down_mat = inputs
        blocks_in = expert_in.astype(jnp.float32).reshape(slot_count, N_CTX, columns)
        blocks_cot = expert_cot.astype(jnp.float32).reshape(slot_count, N_CTX, columns)
        gate_blocks = gate_mat.astype(jnp.float32).reshape(N_CTX, columns, FH)
        up_blocks = up_mat.astype(jnp.float32).reshape(N_CTX, columns, FH)
        down_blocks = down_mat.astype(jnp.float32).reshape(FH, N_CTX, columns)
        gate_pre = rounded_sum(jnp.einsum('scd,cdf->csf', blocks_in, gate_blocks))
        up_pre = rounded_sum(jnp.einsum('scd,cdf->csf', blocks_in, up_blocks))
        back_pre = rounded_sum(jnp.einsum('scd,fcd->csf', blocks_cot, down_blocks))
        hidden_act, grad_gate, grad_up = activate(gate_pre, up_pre, back_pre)
        expert_out = jnp.dot(hidden_act, down_mat, preferred_element_type=jnp.float32).astype(jnp.bfloat16)
        event_grad = (jnp.dot(grad_gate, gate_mat.T, preferred_element_type=jnp.float32)
                      + jnp.dot(grad_up, up_mat.T, preferred_element_type=jnp.float32)).astype(jnp.bfloat16)
        return expert_out, event_grad

    out_buffer, grad_buffer = lax.map(one_expert, (token_buffer, cot_buffer, w_gate, w_up, w_down))
    expert_out = out_buffer[expert_ids, slot_rows].reshape(TOKENS, TOP, D).astype(jnp.float32)
    event_grad = grad_buffer[expert_ids, slot_rows].reshape(TOKENS, TOP, D).astype(jnp.float32)
    mixed = jnp.sum(event_weights[:, :, None] * expert_out, axis=1).astype(jnp.bfloat16)
    token_grad = jnp.sum(event_grad, axis=1).astype(jnp.bfloat16)
    weight_grad = jnp.einsum('td,tkd->tk', cotangent.astype(jnp.float32), expert_out)
    return mixed, token_grad, weight_grad
```

```python
import functools

import jax
import jax.numpy as jnp
from jax import lax
from jax.experimental import pallas as pl
from jax.experimental.pallas import tpu as pltpu
from jax.sharding import PartitionSpec as P


def activate(gate_pre, up_pre, back_pre):
    squash = jax.nn.sigmoid(gate_pre)
    hidden_act = (gate_pre * squash * up_pre).astype(jnp.bfloat16)
    grad_gate = (back_pre * up_pre * squash * (1.0 + gate_pre * (1.0 - squash))).astype(
        jnp.bfloat16
    )
    grad_up = (back_pre * gate_pre * squash).astype(jnp.bfloat16)
    return (hidden_act, grad_gate, grad_up)


def shards(tokens, routes, event_weights, cotangent, w_gate, w_up, w_down):
    owners = lax.axis_size("exp")
    owned, columns, hidden = w_gate.shape
    experts = owned * owners
    rows_here, fanout = routes.shape
    capacity = max(2, 5 * rows_here * fanout // (4 * experts))
    slot_count = owners * capacity
    routes_flat = routes.reshape(-1)
    onehot = (routes_flat[:, None] == jnp.arange(experts, dtype=jnp.int32)[None, :]).astype(
        jnp.int32
    )
    places = jnp.sum((jnp.cumsum(onehot, axis=0) - onehot) * onehot, axis=1)
    targets = routes_flat * capacity + places
    token_rows = jnp.repeat(tokens, fanout, axis=0)
    cot_rows = (
        event_weights.reshape(-1, 1) * jnp.repeat(cotangent.astype(jnp.float32), fanout, axis=0)
    ).astype(jnp.bfloat16)
    send_tokens = jnp.zeros((experts * capacity, columns), jnp.bfloat16).at[targets].set(token_rows)
    send_cots = jnp.zeros((experts * capacity, columns), jnp.bfloat16).at[targets].set(cot_rows)
    send_tokens = send_tokens.reshape(owners, owned * capacity, columns)
    send_cots = send_cots.reshape(owners, owned * capacity, columns)
    recv_tokens, recv_cots = (
        lax.all_to_all(send_tokens, "exp", split_axis=0, concat_axis=0, tiled=True),
        lax.all_to_all(send_cots, "exp", split_axis=0, concat_axis=0, tiled=True),
    )

    def arrange(buffer):
        return (
            buffer.reshape(owners, owned, capacity, columns)
            .transpose(1, 0, 2, 3)
            .reshape(owned, slot_count, columns)
        )

    expert_in = arrange(recv_tokens)
    expert_cot = arrange(recv_cots)
    shares = lax.psum_scatter(
        jnp.stack(
            [
                jnp.einsum("jsd,jdf->fjs", expert_in, w_gate, preferred_element_type=jnp.float32),
                jnp.einsum("jsd,jdf->fjs", expert_in, w_up, preferred_element_type=jnp.float32),
                jnp.einsum("jsd,jfd->fjs", expert_cot, w_down, preferred_element_type=jnp.float32),
            ],
            axis=1,
        ).astype(jnp.bfloat16),
        "ctx",
        scatter_dimension=0,
        tiled=True,
    ).astype(jnp.float32)
    hidden_share, gate_share, up_share = activate(shares[:, 0], shares[:, 1], shares[:, 2])
    hidden_act, grad_gate, grad_up = (
        lax.all_gather(hidden_share, "ctx", axis=0, tiled=True),
        lax.all_gather(gate_share, "ctx", axis=0, tiled=True),
        lax.all_gather(up_share, "ctx", axis=0, tiled=True),
    )
    expert_out = jnp.einsum(
        "fjs,jfd->jsd", hidden_act, w_down, preferred_element_type=jnp.float32
    ).astype(jnp.bfloat16)
    event_grad = (
        jnp.einsum("fjs,jdf->jsd", grad_gate, w_gate, preferred_element_type=jnp.float32)
        + jnp.einsum("fjs,jdf->jsd", grad_up, w_up, preferred_element_type=jnp.float32)
    ).astype(jnp.bfloat16)

    def restore(buffer):
        return (
            buffer.reshape(owned, owners, capacity, columns)
            .transpose(1, 0, 2, 3)
            .reshape(owners, owned * capacity, columns)
        )

    back_out, back_grad = (
        lax.all_to_all(restore(expert_out), "exp", split_axis=0, concat_axis=0, tiled=True),
        lax.all_to_all(restore(event_grad), "exp", split_axis=0, concat_axis=0, tiled=True),
    )
    out_rows = (
        back_out.reshape(experts * capacity, columns)[targets]
        .reshape(rows_here, fanout, columns)
        .astype(jnp.float32)
    )
    grad_rows = (
        back_grad.reshape(experts * capacity, columns)[targets]
        .reshape(rows_here, fanout, columns)
        .astype(jnp.float32)
    )
    mixed = jnp.sum(event_weights[:, :, None] * out_rows, axis=1).astype(jnp.bfloat16)
    token_grad = jnp.sum(grad_rows, axis=1).astype(jnp.bfloat16)
    weight_part = jnp.einsum("td,tkd->tk", cotangent.astype(jnp.float32), out_rows)
    weight_grad = lax.psum(weight_part, "ctx")
    return (mixed, token_grad, weight_grad)


def fused(
    sizes,
    routes_ref, weights_ref, tokens_ref, cot_ref, gate_hbm, up_hbm, down_hbm,
    mixed_ref, grad_ref, wgrad_ref,
    gate_w, up_w, down_w, x_send, x_recv, rt_recv, cots, part, shares, acts, grads, saved,
    out_send, out_recv, eg_send, eg_recv, wg_parts, mix_acc,
    load_sem, x_ssem, x_rsem, rt_ssem, rt_rsem, far_up, far_down, far_rsem, sib_ssem, sib_rsem,
    rs_ssem, rs_rsem, bk_ssem, bk_rsem, ag_ssem, ag_rsem, gg_ssem, gg_rsem,
    out_ssem, out_rsem, eg_ssem, eg_rsem, wg_ssem, wg_rsem,
):
    owners, splits, capacity, rows, columns, hidden = sizes
    part_f = hidden // splits
    half = rows // 2
    z, c, r = lax.axis_index("exp"), lax.axis_index("ctx"), lax.axis_index("rep")
    bf, f32 = jnp.bfloat16, jnp.float32

    def expert_at(d):
        return lax.rem(z + d, owners)

    def source_at(d):
        return lax.rem(z - d + owners, owners)

    def peer_at(q):
        return lax.rem(c + q, splits)

    def from_peer(q):
        return lax.rem(c - q + splits, splits)

    def remote(src, dst, ssem, rsem, **where):
        return pltpu.make_async_remote_copy(
            src_ref=src, dst_ref=dst, send_sem=ssem, recv_sem=rsem,
            device_id=where, device_id_type=pl.DeviceIdType.MESH,
        )

    loads = [
        pltpu.make_async_copy(gate_hbm.at[0], gate_w, load_sem.at[0]),
        pltpu.make_async_copy(up_hbm.at[0], up_w, load_sem.at[1]),
        pltpu.make_async_copy(down_hbm.at[0], down_w, load_sem.at[2]),
    ]
    for load in loads:
        load.start()

    barrier = pltpu.get_barrier_semaphore()
    for d in range(1, owners):
        pl.semaphore_signal(barrier, inc=1, device_id={"exp": expert_at(d)}, device_id_type=pl.DeviceIdType.MESH)
    for q in range(1, splits):
        pl.semaphore_signal(barrier, inc=1, device_id={"ctx": peer_at(q)}, device_id_type=pl.DeviceIdType.MESH)
    pl.semaphore_signal(barrier, inc=1, device_id={"rep": 1 - r}, device_id_type=pl.DeviceIdType.MESH)

    routes = routes_ref[...]
    event_w = weights_ref[...]
    lane = lax.broadcasted_iota(jnp.int32, (rows, 128), 1)
    eye = (lax.broadcasted_iota(jnp.int32, (rows, rows), 0) == lax.broadcasted_iota(jnp.int32, (rows, rows), 1)).astype(bf)
    upper = (lax.broadcasted_iota(jnp.int32, (rows, rows), 0) < lax.broadcasted_iota(jnp.int32, (rows, rows), 1)).astype(bf)
    lower = (lax.broadcasted_iota(jnp.int32, (rows, rows), 0) > lax.broadcasted_iota(jnp.int32, (rows, rows), 1)).astype(bf)
    named = ((lane == routes[:, 0:1]) | (lane == routes[:, 1:2])).astype(f32)
    named_t = lax.dot_general(named.astype(bf), eye, (((0,), (0,)), ((), ())), preferred_element_type=f32)
    rt_recv[0] = named_t[0:16].astype(bf)
    places = jnp.dot(lower, named.astype(bf), preferred_element_type=f32)

    def picks(named_rows, expert):
        row = lax.broadcasted_iota(jnp.int32, (16, rows), 0)
        pos = jnp.dot(named_rows.astype(bf), upper, preferred_element_type=f32)
        mine = row == expert
        pos_e = jnp.sum(jnp.where(mine, pos, 0.0), axis=0, keepdims=True)
        has_e = jnp.sum(jnp.where(mine, named_rows.astype(f32), 0.0), axis=0, keepdims=True)
        slot = lax.broadcasted_iota(jnp.int32, (capacity, rows), 0).astype(f32)
        return ((slot == pos_e) & (has_e > 0.5)).astype(bf)

    pl.semaphore_wait(barrier, owners + splits - 1)

    x_copies, rt_copies = [], []
    for d in list(range(1, owners)) + [0]:
        block = jnp.dot(picks(rt_recv[0], expert_at(d)), tokens_ref[...], preferred_element_type=f32).astype(bf)
        if d == 0:
            x_recv[0] = block
            continue
        x_send[d] = block
        rt = remote(rt_recv.at[0], rt_recv.at[d], rt_ssem.at[d], rt_rsem.at[d], exp=expert_at(d))
        cp = remote(x_send.at[d], x_recv.at[d], x_ssem.at[d], x_rsem.at[d], exp=expert_at(d))
        rt.start()
        cp.start()
        rt_copies.append(rt)
        x_copies.append(cp)

    my_half = pl.ds(pl.multiple_of(r * half, half), half)

    def far(src, j, going_up):
        sem = far_up if going_up else far_down
        return remote(src, cots.at[j, my_half], sem.at[j], far_rsem.at[j], exp=z + (1 if going_up else -1))

    def sibling(j):
        return remote(cots.at[j, my_half], cots.at[j, my_half], sib_ssem.at[j], sib_rsem.at[j], rep=1 - r)

    @pl.when(z < owners - 1)
    def _():
        far(cot_ref.at[my_half], z, True).start()

    @pl.when(z > 0)
    def _():
        far(cot_ref.at[my_half], z, False).start()

    cots[z] = cot_ref[...]

    def pass_on(d):
        @pl.when(z - d >= 0)
        def _():
            j = z - d
            far(cots.at[j, my_half], j, True).wait_recv()

            @pl.when(z < owners - 1)
            def _():
                far(cots.at[j, my_half], j, True).start()

            sibling(j).start()

        @pl.when(z + d < owners)
        def _():
            j = z + d
            far(cots.at[j, my_half], j, False).wait_recv()

            @pl.when(z > 0)
            def _():
                far(cots.at[j, my_half], j, False).start()

            sibling(j).start()

    for load in loads:
        load.wait()

    def slices(p):
        return slice(p * part_f, (p + 1) * part_f)

    def first(d):
        x = x_recv[d]
        for p in range(splits):
            part[d, p, 0:capacity] = jnp.dot(x, gate_w[:, slices(p)], preferred_element_type=f32).astype(bf)
            part[d, p, capacity:2 * capacity] = jnp.dot(x, up_w[:, slices(p)], preferred_element_type=f32).astype(bf)

    def back(d):
        rows_in = jnp.dot(picks(rt_recv[d], z), cots[source_at(d)], preferred_element_type=f32).astype(bf)
        for p in range(splits):
            part[d, p, 2 * capacity:3 * capacity] = lax.dot_general(
                rows_in, down_w[slices(p), :], (((1,), (1,)), ((), ())), preferred_element_type=f32
            ).astype(bf)

    def rs(d, q):
        at = pl.ds(0, 2 * capacity)
        return remote(part.at[d, peer_at(q), at], shares.at[d, q, at], rs_ssem.at[d, q], rs_rsem.at[d, q], ctx=peer_at(q))

    def bk(d, q):
        at = pl.ds(2 * capacity, capacity)
        return remote(part.at[d, peer_at(q), at], shares.at[d, q, at], bk_ssem.at[d, q], bk_rsem.at[d, q], ctx=peer_at(q))

    def ag(d, q):
        return remote(acts.at[d, c], acts.at[d, c], ag_ssem.at[d, q], ag_rsem.at[d, q], ctx=peer_at(q))

    def gg(d, q):
        return remote(grads.at[d, c], grads.at[d, c], gg_ssem.at[d, q], gg_rsem.at[d, q], ctx=peer_at(q))

    def out(d):
        return remote(out_send.at[d], out_recv.at[d], out_ssem.at[d], out_rsem.at[d], exp=source_at(d))

    def eg(d):
        return remote(eg_send.at[d], eg_recv.at[d], eg_ssem.at[d], eg_rsem.at[d], exp=source_at(d))

    others = range(1, splits)

    for d in range(owners):
        if d > 0:
            x_copies[d - 1].wait_recv()
            rt_copies[d - 1].wait_recv()
        first(d)
        for q in others:
            rs(d, q).start()
        if d > 0:
            pass_on(d)

    def activate_block(d):
        for q in others:
            rs(d, q).wait_recv()
        both = part[d, c, 0:2 * capacity].astype(f32)
        for q in others:
            both = both + shares[d, q, 0:2 * capacity].astype(f32)
        saved[d] = both
        gate_pre, up_pre = both[0:capacity], both[capacity:]
        acts[d, c] = (gate_pre * jax.nn.sigmoid(gate_pre) * up_pre).astype(bf)
        for q in others:
            ag(d, q).start()

    def back_block(d):
        if d > 0:
            @pl.when(z >= d)
            def _():
                sibling(z - d).wait_recv()

            @pl.when(z < d)
            def _():
                sibling(z - d + owners).wait_recv()
        back(d)
        for q in others:
            bk(d, q).start()

    for d in range(owners):
        activate_block(d)
        back_block(d)

    def out_block(d):
        for q in others:
            ag(d, q).wait_recv()
        target = out_recv if d == 0 else out_send
        act = jnp.concatenate([acts[d, p] for p in range(splits)], axis=1)
        target[d] = jnp.dot(act, down_w[...], preferred_element_type=f32).astype(bf)
        if d > 0:
            out(d).start()

    def grad_block(d):
        for q in others:
            bk(d, q).wait_recv()
        back_pre = part[d, c, 2 * capacity:].astype(f32)
        for q in others:
            back_pre = back_pre + shares[d, q, 2 * capacity:].astype(f32)
        gate_pre, up_pre = saved[d, 0:capacity], saved[d, capacity:]
        squash = jax.nn.sigmoid(gate_pre)
        grads[d, c, 0:capacity] = (back_pre * up_pre * squash * (1.0 + gate_pre * (1.0 - squash))).astype(bf)
        grads[d, c, capacity:] = (back_pre * gate_pre * squash).astype(bf)
        for q in others:
            gg(d, q).start()

    order = list(range(1, owners)) + [0]
    for d in order:
        out_block(d)
        grad_block(d)

    def eg_block(d):
        for q in others:
            gg(d, q).wait_recv()
        target = eg_recv if d == 0 else eg_send
        gate_g = jnp.concatenate([grads[d, p, 0:capacity] for p in range(splits)], axis=1)
        up_g = jnp.concatenate([grads[d, p, capacity:] for p in range(splits)], axis=1)
        step = 256 if columns % 256 == 0 else columns
        for n in range(0, columns, step):
            nt = (((1,), (1,)), ((), ()))
            target[d, :, n:n + step] = (
                lax.dot_general(gate_g, gate_w[n:n + step], nt, preferred_element_type=f32)
                + lax.dot_general(up_g, up_w[n:n + step], nt, preferred_element_type=f32)
            ).astype(bf)
        if d > 0:
            eg(d).start()

    for d in order:
        eg_block(d)

    def chosen(d):
        expert = expert_at(d)
        mine = lane == expert
        pos = jnp.sum(jnp.where(mine, places, 0.0), axis=1, keepdims=True)
        has = jnp.sum(jnp.where(mine, named, 0.0), axis=1, keepdims=True)
        weight = jnp.sum(jnp.where(routes == expert, event_w, 0.0), axis=1, keepdims=True)
        slot = lax.broadcasted_iota(jnp.int32, (rows, capacity), 1).astype(f32)
        return ((slot == pos) & (has > 0.5)).astype(bf), weight, expert

    step = 256 if columns % 256 == 0 else columns

    def collect(d, recv, into, last, with_dot):
        pick, weight, expert = chosen(d)
        dots = jnp.zeros((rows, 1), f32)
        for n in range(0, columns, step):
            at = slice(n, n + step)
            row = jnp.dot(pick, recv[d, :, at], preferred_element_type=f32)
            total = weight * row
            if d > 0:
                total = total + mix_acc[:, at]
            if last:
                into[:, at] = total.astype(bf)
            else:
                mix_acc[:, at] = total
            if with_dot:
                dots = dots + jnp.sum(row * cot_ref[:, at].astype(f32), axis=1, keepdims=True)
        return dots, expert

    acc = jnp.zeros((rows, 128), f32)
    wide = jnp.where(lane == 0, routes[:, 0:1], jnp.where(lane == 1, routes[:, 1:2], -1))
    for d in range(owners):
        if d > 0:
            out(d).wait_recv()
        dots, expert = collect(d, out_recv, mixed_ref, d == owners - 1, True)
        acc = acc + jnp.where(wide == expert, dots, 0.0)
    wg_parts[0] = acc

    def wg(q):
        return remote(wg_parts.at[0], wg_parts.at[q], wg_ssem.at[q], wg_rsem.at[q], ctx=peer_at(q))

    for q in others:
        wg(q).start()
    for d in range(owners):
        if d > 0:
            eg(d).wait_recv()
        collect(d, eg_recv, grad_ref, d == owners - 1, False)
    for q in others:
        wg(q).wait_recv()
        acc = acc + wg_parts[q]
    wgrad_ref[...] = acc[:, 0:2]

    for d in range(1, owners):
        x_copies[d - 1].wait_send()
        rt_copies[d - 1].wait_send()
        out(d).wait_send()
        eg(d).wait_send()
    for q in others:
        wg(q).wait_send()
        for d in range(owners):
            rs(d, q).wait_send()
            bk(d, q).wait_send()
            ag(d, q).wait_send()
            gg(d, q).wait_send()

    @pl.when(z < owners - 1)
    def _():
        far(cot_ref.at[my_half], z, True).wait_send()

    @pl.when(z > 0)
    def _():
        far(cot_ref.at[my_half], z, False).wait_send()

    for d in range(1, owners):
        @pl.when(z - d >= 0)
        def _():
            @pl.when(z < owners - 1)
            def _():
                far(cots.at[z - d, my_half], z - d, True).wait_send()

            sibling(z - d).wait_send()

        @pl.when(z + d < owners)
        def _():
            @pl.when(z > 0)
            def _():
                far(cots.at[z + d, my_half], z + d, False).wait_send()

            sibling(z + d).wait_send()


def shards_fused(tokens, routes, event_weights, cotangent, w_gate, w_up, w_down):
    owners, splits = lax.axis_size("exp"), lax.axis_size("ctx")
    _, columns, hidden = w_gate.shape
    rows, fanout = routes.shape
    capacity = max(2, 5 * rows * fanout // (4 * owners))
    part_f = hidden // splits
    sizes = (owners, splits, capacity, rows, columns, hidden)
    bf, f32 = jnp.bfloat16, jnp.float32
    vmem, dma = pltpu.VMEM, pltpu.SemaphoreType.DMA
    full = pl.BlockSpec(memory_space=pltpu.VMEM)
    anywhere = pl.BlockSpec(memory_space=pl.ANY)
    per_block = dma((owners,))
    per_pair = dma((owners, splits))
    moved = owners * capacity * columns
    return pl.pallas_call(
        functools.partial(fused, sizes),
        out_shape=(
            jax.ShapeDtypeStruct((rows, columns), bf),
            jax.ShapeDtypeStruct((rows, columns), bf),
            jax.ShapeDtypeStruct((rows, fanout), f32),
        ),
        in_specs=[full, full, full, full, anywhere, anywhere, anywhere],
        out_specs=(full, full, full),
        scratch_shapes=[
            vmem((columns, hidden), bf), vmem((columns, hidden), bf), vmem((hidden, columns), bf),
            vmem((owners, capacity, columns), bf), vmem((owners, capacity, columns), bf),
            vmem((owners, 16, rows), bf),
            vmem((owners, rows, columns), bf),
            vmem((owners, splits, 3 * capacity, part_f), bf),
            vmem((owners, splits, 3 * capacity, part_f), bf),
            vmem((owners, splits, capacity, part_f), bf),
            vmem((owners, splits, 2 * capacity, part_f), bf),
            vmem((owners, 2 * capacity, part_f), f32),
            vmem((owners, capacity, columns), bf), vmem((owners, capacity, columns), bf),
            vmem((owners, capacity, columns), bf), vmem((owners, capacity, columns), bf),
            vmem((splits, rows, 128), f32),
            vmem((rows, columns), f32),
            dma((3,)), per_block, per_block, per_block, per_block,
            per_block, per_block, per_block, per_block, per_block,
            per_pair, per_pair, per_pair, per_pair, per_pair, per_pair, per_pair, per_pair,
            per_block, per_block, per_block, per_block, dma((splits,)), dma((splits,)),
        ],
        compiler_params=pltpu.CompilerParams(
            collective_id=0, has_side_effects=True, vmem_limit_bytes=56 * 1024 * 1024
        ),
        cost_estimate=pl.CostEstimate(
            flops=12 * moved * hidden, bytes_accessed=6 * columns * hidden, transcendentals=0
        ),
    )(routes, event_weights, tokens, cotangent, w_gate, w_up, w_down)


def fits(mesh, w_gate, routes):
    owners, splits, cores = mesh.shape["exp"], mesh.shape["ctx"], mesh.shape["rep"]
    experts, depth, hidden = w_gate.shape
    rows, fanout = routes.shape[0] // (owners * cores), routes.shape[1]
    capacity = max(2, 5 * rows * fanout // (4 * experts))
    columns = depth // splits
    return (
        experts == owners and 1 < owners <= 8 and splits > 1 and cores == 2 and fanout == 2
        and rows == 128 and capacity % 16 == 0 and columns % 128 == 0 and hidden % (128 * splits) == 0
        and 6 * columns * hidden <= 16 * 1024 * 1024
    )


def solution(mesh):
    in_specs = (
        P(("rep", "exp"), "ctx"),
        P(("rep", "exp"), None),
        P(("rep", "exp"), None),
        P("exp", "ctx"),
        P("exp", "ctx", None),
        P("exp", "ctx", None),
        P("exp", None, "ctx"),
    )
    out_specs = (P(("rep", "exp"), "ctx"), P(("rep", "exp"), "ctx"), P(("rep", "exp"), None))

    def run(tokens, routes, event_weights, cotangent, w_gate, w_up, w_down):
        body = shards_fused if fits(mesh, w_gate, routes) else shards
        mapped = jax.shard_map(body, mesh=mesh, in_specs=in_specs, out_specs=out_specs, check_vma=False)
        return mapped(tokens, routes, event_weights, cotangent, w_gate, w_up, w_down)

    return run
```

```python
import functools

import jax
import jax.numpy as jnp
from jax import lax
from jax.experimental import pallas as pl
from jax.experimental.pallas import tpu as pltpu
from jax.sharding import PartitionSpec as P


def activate(gate_pre, up_pre, back_pre):
    squash = jax.nn.sigmoid(gate_pre)
    hidden_act = (gate_pre * squash * up_pre).astype(jnp.bfloat16)
    grad_gate = (back_pre * up_pre * squash * (1.0 + gate_pre * (1.0 - squash))).astype(
        jnp.bfloat16
    )
    grad_up = (back_pre * gate_pre * squash).astype(jnp.bfloat16)
    return (hidden_act, grad_gate, grad_up)


def shards(tokens, routes, event_weights, cotangent, w_gate, w_up, w_down):
    owners = lax.axis_size("exp")
    owned, columns, hidden = w_gate.shape
    experts = owned * owners
    rows_here, fanout = routes.shape
    capacity = max(2, 5 * rows_here * fanout // (4 * experts))
    slot_count = owners * capacity
    routes_flat = routes.reshape(-1)
    onehot = (routes_flat[:, None] == jnp.arange(experts, dtype=jnp.int32)[None, :]).astype(
        jnp.int32
    )
    places = jnp.sum((jnp.cumsum(onehot, axis=0) - onehot) * onehot, axis=1)
    targets = routes_flat * capacity + places
    token_rows = jnp.repeat(tokens, fanout, axis=0)
    cot_rows = (
        event_weights.reshape(-1, 1) * jnp.repeat(cotangent.astype(jnp.float32), fanout, axis=0)
    ).astype(jnp.bfloat16)
    send_tokens = jnp.zeros((experts * capacity, columns), jnp.bfloat16).at[targets].set(token_rows)
    send_cots = jnp.zeros((experts * capacity, columns), jnp.bfloat16).at[targets].set(cot_rows)
    send_tokens = send_tokens.reshape(owners, owned * capacity, columns)
    send_cots = send_cots.reshape(owners, owned * capacity, columns)
    recv_tokens, recv_cots = (
        lax.all_to_all(send_tokens, "exp", split_axis=0, concat_axis=0, tiled=True),
        lax.all_to_all(send_cots, "exp", split_axis=0, concat_axis=0, tiled=True),
    )

    def arrange(buffer):
        return (
            buffer.reshape(owners, owned, capacity, columns)
            .transpose(1, 0, 2, 3)
            .reshape(owned, slot_count, columns)
        )

    expert_in = arrange(recv_tokens)
    expert_cot = arrange(recv_cots)
    shares = lax.psum_scatter(
        jnp.stack(
            [
                jnp.einsum("jsd,jdf->fjs", expert_in, w_gate, preferred_element_type=jnp.float32),
                jnp.einsum("jsd,jdf->fjs", expert_in, w_up, preferred_element_type=jnp.float32),
                jnp.einsum("jsd,jfd->fjs", expert_cot, w_down, preferred_element_type=jnp.float32),
            ],
            axis=1,
        ).astype(jnp.bfloat16),
        "ctx",
        scatter_dimension=0,
        tiled=True,
    ).astype(jnp.float32)
    hidden_share, gate_share, up_share = activate(shares[:, 0], shares[:, 1], shares[:, 2])
    hidden_act, grad_gate, grad_up = (
        lax.all_gather(hidden_share, "ctx", axis=0, tiled=True),
        lax.all_gather(gate_share, "ctx", axis=0, tiled=True),
        lax.all_gather(up_share, "ctx", axis=0, tiled=True),
    )
    expert_out = jnp.einsum(
        "fjs,jfd->jsd", hidden_act, w_down, preferred_element_type=jnp.float32
    ).astype(jnp.bfloat16)
    event_grad = (
        jnp.einsum("fjs,jdf->jsd", grad_gate, w_gate, preferred_element_type=jnp.float32)
        + jnp.einsum("fjs,jdf->jsd", grad_up, w_up, preferred_element_type=jnp.float32)
    ).astype(jnp.bfloat16)

    def restore(buffer):
        return (
            buffer.reshape(owned, owners, capacity, columns)
            .transpose(1, 0, 2, 3)
            .reshape(owners, owned * capacity, columns)
        )

    back_out, back_grad = (
        lax.all_to_all(restore(expert_out), "exp", split_axis=0, concat_axis=0, tiled=True),
        lax.all_to_all(restore(event_grad), "exp", split_axis=0, concat_axis=0, tiled=True),
    )
    out_rows = (
        back_out.reshape(experts * capacity, columns)[targets]
        .reshape(rows_here, fanout, columns)
        .astype(jnp.float32)
    )
    grad_rows = (
        back_grad.reshape(experts * capacity, columns)[targets]
        .reshape(rows_here, fanout, columns)
        .astype(jnp.float32)
    )
    mixed = jnp.sum(event_weights[:, :, None] * out_rows, axis=1).astype(jnp.bfloat16)
    token_grad = jnp.sum(grad_rows, axis=1).astype(jnp.bfloat16)
    weight_part = jnp.einsum("td,tkd->tk", cotangent.astype(jnp.float32), out_rows)
    weight_grad = lax.psum(weight_part, "ctx")
    return (mixed, token_grad, weight_grad)


def fused(
    sizes,
    routes_ref, weights_ref, tokens_ref, cot_ref, gate_hbm, up_hbm, down_hbm,
    mixed_ref, grad_ref, wgrad_ref,
    gate_w, up_w, down_w, x_send, x_recv, rt_recv, cots, part, shares, acts, grads, saved,
    out_send, out_recv, eg_send, eg_recv, wg_parts, mix_acc,
    load_sem, x_ssem, x_rsem, rt_ssem, rt_rsem, far_up, far_down, far_rsem, sib_ssem, sib_rsem,
    rs_ssem, rs_rsem, bk_ssem, bk_rsem, ag_ssem, ag_rsem, gg_ssem, gg_rsem,
    out_ssem, out_rsem, eg_ssem, eg_rsem, wg_ssem, wg_rsem,
):
    owners, splits, capacity, rows, columns, hidden = sizes
    part_f = hidden // splits
    half = rows // 2
    z, c, r = lax.axis_index("exp"), lax.axis_index("ctx"), lax.axis_index("rep")
    bf, f32 = jnp.bfloat16, jnp.float32

    def expert_at(d):
        return lax.rem(z + d, owners)

    def source_at(d):
        return lax.rem(z - d + owners, owners)

    def peer_at(q):
        return lax.rem(c + q, splits)

    def from_peer(q):
        return lax.rem(c - q + splits, splits)

    def remote(src, dst, ssem, rsem, **where):
        return pltpu.make_async_remote_copy(
            src_ref=src, dst_ref=dst, send_sem=ssem, recv_sem=rsem,
            device_id=where, device_id_type=pl.DeviceIdType.MESH,
        )

    loads = [
        pltpu.make_async_copy(gate_hbm.at[0], gate_w, load_sem.at[0]),
        pltpu.make_async_copy(up_hbm.at[0], up_w, load_sem.at[1]),
        pltpu.make_async_copy(down_hbm.at[0], down_w, load_sem.at[2]),
    ]
    for load in loads:
        load.start()

    barrier = pltpu.get_barrier_semaphore()
    for d in range(1, owners):
        pl.semaphore_signal(barrier, inc=1, device_id={"exp": expert_at(d)}, device_id_type=pl.DeviceIdType.MESH)
    for q in range(1, splits):
        pl.semaphore_signal(barrier, inc=1, device_id={"ctx": peer_at(q)}, device_id_type=pl.DeviceIdType.MESH)
    pl.semaphore_signal(barrier, inc=1, device_id={"rep": 1 - r}, device_id_type=pl.DeviceIdType.MESH)

    routes = routes_ref[...]
    event_w = weights_ref[...]
    row_i = lax.broadcasted_iota(jnp.int32, (rows, rows), 0)
    col_i = lax.broadcasted_iota(jnp.int32, (rows, rows), 1)
    eye, upper, lower = row_i == col_i, (row_i < col_i).astype(bf), (row_i > col_i).astype(bf)
    experts_i = lax.broadcasted_iota(jnp.int32, (16, rows), 0)
    named_t = ((experts_i == routes[0:1]) | (experts_i == routes[1:2])).astype(f32).astype(bf)
    rt_recv[0] = named_t
    named = lax.dot_general(eye.astype(f32).astype(bf), named_t, (((1,), (1,)), ((), ())), preferred_element_type=f32)
    places = jnp.dot(lower, named.astype(bf), preferred_element_type=f32)

    def line(i):
        near = jnp.minimum(z, owners - 1 - z)
        paired = i <= 2 * near
        distance = jnp.where(paired, (i + 1) // 2, i - near)
        ahead = jnp.where(paired, i % 2 == 0, z < owners - 1 - z)
        other = z + jnp.where(ahead, distance, -distance)
        return other, lax.rem(z - other + owners, owners), lax.rem(other - z + owners, owners)

    def picks(named_rows, expert):
        pos = jnp.dot(named_rows, upper, preferred_element_type=f32)
        mine = experts_i == expert
        pos_e = jnp.sum(jnp.where(mine, pos, 0.0), axis=0, keepdims=True)
        has_e = jnp.sum(jnp.where(mine, named_rows.astype(f32), 0.0), axis=0, keepdims=True)
        slot = lax.broadcasted_iota(jnp.int32, (capacity, rows), 0).astype(f32)
        return ((slot == pos_e) & (has_e > 0.5)).astype(bf)

    pl.semaphore_wait(barrier, owners + splits - 1)

    steps = range(1, owners)

    def rt(i):
        other, _, d = line(i)
        return remote(rt_recv.at[0], rt_recv.at[d], rt_ssem.at[i], rt_rsem.at[d], exp=other)

    def send_x(i):
        other, _, d = line(i)
        return remote(x_send.at[i], x_recv.at[d], x_ssem.at[i], x_rsem.at[d], exp=other)

    def got_x(i):
        other, d, _ = line(i)
        remote(rt_recv.at[0], rt_recv.at[d], rt_ssem.at[i], rt_rsem.at[d], exp=other).wait_recv()
        remote(x_send.at[i], x_recv.at[d], x_ssem.at[i], x_rsem.at[d], exp=other).wait_recv()
        return d

    for i in steps:
        rt(i).start()
    for i in steps:
        x_send[i] = jnp.dot(picks(rt_recv[0], line(i)[0]), tokens_ref[...], preferred_element_type=f32).astype(bf)
        send_x(i).start()

    my_half = pl.ds(pl.multiple_of(r * half, half), half)

    def far(src, j, going_up):
        sem = far_up if going_up else far_down
        return remote(src, cots.at[j, my_half], sem.at[j], far_rsem.at[j], exp=z + (1 if going_up else -1))

    def sibling(j):
        return remote(cots.at[j, my_half], cots.at[j, my_half], sib_ssem.at[j], sib_rsem.at[j], rep=1 - r)

    @pl.when(z < owners - 1)
    def _():
        far(cot_ref.at[my_half], z, True).start()

    @pl.when(z > 0)
    def _():
        far(cot_ref.at[my_half], z, False).start()

    cots[z] = cot_ref[...]
    x_recv[0] = jnp.dot(picks(rt_recv[0], z), tokens_ref[...], preferred_element_type=f32).astype(bf)

    def pass_on(d):
        @pl.when(z - d >= 0)
        def _():
            j = z - d
            far(cots.at[j, my_half], j, True).wait_recv()

            @pl.when(z < owners - 1)
            def _():
                far(cots.at[j, my_half], j, True).start()

            sibling(j).start()

        @pl.when(z + d < owners)
        def _():
            j = z + d
            far(cots.at[j, my_half], j, False).wait_recv()

            @pl.when(z > 0)
            def _():
                far(cots.at[j, my_half], j, False).start()

            sibling(j).start()

    for load in loads:
        load.wait()

    def slices(p):
        return slice(p * part_f, (p + 1) * part_f)

    def first(d):
        x = x_recv[d]
        for p in range(splits):
            part[d, p, 0:capacity] = jnp.dot(x, gate_w[:, slices(p)], preferred_element_type=f32).astype(bf)
            part[d, p, capacity:2 * capacity] = jnp.dot(x, up_w[:, slices(p)], preferred_element_type=f32).astype(bf)

    def back(d):
        rows_in = jnp.dot(picks(rt_recv[d], z), cots[source_at(d)], preferred_element_type=f32).astype(bf)
        for p in range(splits):
            part[d, p, 2 * capacity:3 * capacity] = lax.dot_general(
                rows_in, down_w[slices(p), :], (((1,), (1,)), ((), ())), preferred_element_type=f32
            ).astype(bf)

    def rs(d, q):
        at = pl.ds(0, 2 * capacity)
        return remote(part.at[d, peer_at(q), at], shares.at[d, q, at], rs_ssem.at[d, q], rs_rsem.at[d, q], ctx=peer_at(q))

    def bk(d, q):
        at = pl.ds(2 * capacity, capacity)
        return remote(part.at[d, peer_at(q), at], shares.at[d, q, at], bk_ssem.at[d, q], bk_rsem.at[d, q], ctx=peer_at(q))

    def ag(d, q):
        return remote(acts.at[d, c], acts.at[d, c], ag_ssem.at[d, q], ag_rsem.at[d, q], ctx=peer_at(q))

    def gg(d, q):
        return remote(grads.at[d, c], grads.at[d, c], gg_ssem.at[d, q], gg_rsem.at[d, q], ctx=peer_at(q))

    def out(i):
        other, d, _ = line(i)
        return remote(out_send.at[i], out_recv.at[d], out_ssem.at[i], out_rsem.at[d], exp=other)

    def eg(i):
        other, d, _ = line(i)
        return remote(eg_send.at[i], eg_recv.at[d], eg_ssem.at[i], eg_rsem.at[d], exp=other)

    others = range(1, splits)

    def activate_block(d):
        for q in others:
            rs(d, q).wait_recv()
        both = part[d, c, 0:2 * capacity].astype(f32)
        for q in others:
            both = both + shares[d, q, 0:2 * capacity].astype(f32)
        saved[d] = both
        gate_pre, up_pre = both[0:capacity], both[capacity:]
        acts[d, c] = (gate_pre * jax.nn.sigmoid(gate_pre) * up_pre).astype(bf)
        for q in others:
            ag(d, q).start()

    def back_block(i):
        d = 0
        if i > 0:
            other, d, _ = line(i)
            sibling(other).wait_recv()
        back(d)
        for q in others:
            bk(d, q).start()

    def first_block(i):
        d = got_x(i) if i else 0
        first(d)
        for q in others:
            rs(d, q).start()

    def slot(i):
        return line(i)[1] if i else 0

    def out_block(i):
        d = slot(i)
        for q in others:
            ag(d, q).wait_recv()
        act = jnp.concatenate([acts[d, p] for p in range(splits)], axis=1)
        target = out_send if i else out_recv
        target[i] = jnp.dot(act, down_w[...], preferred_element_type=f32).astype(bf)
        if i:
            out(i).start()

    def grad_block(d):
        for q in others:
            bk(d, q).wait_recv()
        back_pre = part[d, c, 2 * capacity:].astype(f32)
        for q in others:
            back_pre = back_pre + shares[d, q, 2 * capacity:].astype(f32)
        gate_pre, up_pre = saved[d, 0:capacity], saved[d, capacity:]
        squash = jax.nn.sigmoid(gate_pre)
        grads[d, c, 0:capacity] = (back_pre * up_pre * squash * (1.0 + gate_pre * (1.0 - squash))).astype(bf)
        grads[d, c, capacity:] = (back_pre * gate_pre * squash).astype(bf)
        for q in others:
            gg(d, q).start()

    def eg_block(i):
        d = slot(i)
        for q in others:
            gg(d, q).wait_recv()
        target = eg_send if i else eg_recv
        gate_g = jnp.concatenate([grads[d, p, 0:capacity] for p in range(splits)], axis=1)
        up_g = jnp.concatenate([grads[d, p, capacity:] for p in range(splits)], axis=1)
        step = 256 if columns % 256 == 0 else columns
        for n in range(0, columns, step):
            nt = (((1,), (1,)), ((), ()))
            target[i, :, n:n + step] = (
                lax.dot_general(gate_g, gate_w[n:n + step], nt, preferred_element_type=f32)
                + lax.dot_general(up_g, up_w[n:n + step], nt, preferred_element_type=f32)
            ).astype(bf)
        if i:
            eg(i).start()

    first_block(0)
    back_block(0)
    last = owners - 1
    for i in steps:
        first_block(i)
        activate_block(slot(i - 1))
        if i > 1:
            out_block(i - 1)
        pass_on(i)
    activate_block(slot(last))
    for i in steps:
        back_block(i)
        if i == 1:
            out_block(last)
    grad_block(0)
    for i in steps:
        grad_block(slot(i))
        if i > 1:
            eg_block(i - 1)
    eg_block(last)
    out_block(0)
    eg_block(0)

    def weight_row(expert):
        return jnp.sum(jnp.where(routes == expert, event_w, 0.0), axis=0, keepdims=True)

    def chosen(expert):
        mine = lax.broadcasted_iota(jnp.int32, (rows, 16), 1) == expert
        pos = jnp.sum(jnp.where(mine, places, 0.0), axis=1, keepdims=True)
        has = jnp.sum(jnp.where(mine, named, 0.0), axis=1, keepdims=True)
        weight = jnp.sum(jnp.where(eye, weight_row(expert), 0.0), axis=1, keepdims=True)
        place = lax.broadcasted_iota(jnp.int32, (rows, capacity), 1).astype(f32)
        return ((place == pos) & (has > 0.5)).astype(bf), weight

    step = 256 if columns % 256 == 0 else columns

    def collect(i, recv, into, with_dot):
        expert, d = z, 0
        if i:
            expert, _, d = line(i)
        pick, weight = chosen(expert)
        dots = jnp.zeros((rows, 1), f32)
        for n in range(0, columns, step):
            at = slice(n, n + step)
            row = jnp.dot(pick, recv[d, :, at], preferred_element_type=f32)
            total = weight * row
            if i > 0:
                total = total + mix_acc[:, at]
            if i == last:
                into[:, at] = total.astype(bf)
            else:
                mix_acc[:, at] = total
            if with_dot:
                dots = dots + jnp.sum(row * cot_ref[:, at].astype(f32), axis=1, keepdims=True)
        if not with_dot:
            return None
        return jnp.where(routes == expert, jnp.sum(jnp.where(eye, dots, 0.0), axis=0, keepdims=True), 0.0)

    def wg(q):
        return remote(wg_parts.at[0], wg_parts.at[q], wg_ssem.at[q], wg_rsem.at[q], ctx=peer_at(q))

    acc = jnp.zeros(routes.shape, f32)
    for i in range(owners):
        if i:
            remote(out_send.at[i], out_recv.at[line(i)[2]], out_ssem.at[i], out_rsem.at[line(i)[2]], exp=line(i)[0]).wait_recv()
        acc = acc + collect(i, out_recv, mixed_ref, True)
    wg_parts[0, 0:routes.shape[0]] = acc
    wg_parts[0, routes.shape[0]:] = jnp.zeros((8 - routes.shape[0], rows), f32)
    for q in others:
        wg(q).start()
    for i in range(owners):
        if i:
            remote(eg_send.at[i], eg_recv.at[line(i)[2]], eg_ssem.at[i], eg_rsem.at[line(i)[2]], exp=line(i)[0]).wait_recv()
        collect(i, eg_recv, grad_ref, False)
    for q in others:
        wg(q).wait_recv()
        acc = acc + wg_parts[q, 0:routes.shape[0]]
    wgrad_ref[...] = acc

    for i in steps:
        send_x(i).wait_send()
        rt(i).wait_send()
        out(i).wait_send()
        eg(i).wait_send()
    for q in others:
        wg(q).wait_send()
        for d in range(owners):
            rs(d, q).wait_send()
            bk(d, q).wait_send()
            ag(d, q).wait_send()
            gg(d, q).wait_send()

    @pl.when(z < owners - 1)
    def _():
        far(cot_ref.at[my_half], z, True).wait_send()

    @pl.when(z > 0)
    def _():
        far(cot_ref.at[my_half], z, False).wait_send()

    for d in range(1, owners):
        @pl.when(z - d >= 0)
        def _():
            @pl.when(z < owners - 1)
            def _():
                far(cots.at[z - d, my_half], z - d, True).wait_send()

            sibling(z - d).wait_send()

        @pl.when(z + d < owners)
        def _():
            @pl.when(z > 0)
            def _():
                far(cots.at[z + d, my_half], z + d, False).wait_send()

            sibling(z + d).wait_send()


def hand_over(*refs):
    for source, target in zip(refs[:3], refs[3:]):
        target[...] = source[...]


def shards_fused(tokens, routes, event_weights, cotangent, w_gate, w_up, w_down):
    owners, splits = lax.axis_size("exp"), lax.axis_size("ctx")
    _, columns, hidden = w_gate.shape
    rows, fanout = routes.shape
    capacity = max(2, 5 * rows * fanout // (4 * owners))
    part_f = hidden // splits
    sizes = (owners, splits, capacity, rows, columns, hidden)
    bf, f32 = jnp.bfloat16, jnp.float32
    vmem, dma = pltpu.VMEM, pltpu.SemaphoreType.DMA
    full = pl.BlockSpec(memory_space=pltpu.VMEM)
    anywhere = pl.BlockSpec(memory_space=pl.ANY)
    per_block = dma((owners,))
    per_pair = dma((owners, splits))
    moved = owners * capacity * columns
    results = pl.pallas_call(
        functools.partial(fused, sizes),
        out_shape=(
            jax.ShapeDtypeStruct((rows, columns), bf),
            jax.ShapeDtypeStruct((rows, columns), bf),
            jax.ShapeDtypeStruct((fanout, rows), f32),
        ),
        in_specs=[full, full, full, full, anywhere, anywhere, anywhere],
        out_specs=(full, full, full),
        scratch_shapes=[
            vmem((columns, hidden), bf), vmem((columns, hidden), bf), vmem((hidden, columns), bf),
            vmem((owners, capacity, columns), bf), vmem((owners, capacity, columns), bf),
            vmem((owners, 16, rows), bf),
            vmem((owners, rows, columns), bf),
            vmem((owners, splits, 3 * capacity, part_f), bf),
            vmem((owners, splits, 3 * capacity, part_f), bf),
            vmem((owners, splits, capacity, part_f), bf),
            vmem((owners, splits, 2 * capacity, part_f), bf),
            vmem((owners, 2 * capacity, part_f), f32),
            vmem((owners, capacity, columns), bf), vmem((owners, capacity, columns), bf),
            vmem((owners, capacity, columns), bf), vmem((owners, capacity, columns), bf),
            vmem((splits, 8, rows), f32),
            vmem((rows, columns), f32),
            dma((3,)), per_block, per_block, per_block, per_block,
            per_block, per_block, per_block, per_block, per_block,
            per_pair, per_pair, per_pair, per_pair, per_pair, per_pair, per_pair, per_pair,
            per_block, per_block, per_block, per_block, dma((splits,)), dma((splits,)),
        ],
        compiler_params=pltpu.CompilerParams(
            collective_id=0, has_side_effects=True, vmem_limit_bytes=56 * 1024 * 1024
        ),
        cost_estimate=pl.CostEstimate(
            flops=12 * moved * hidden, bytes_accessed=6 * columns * hidden, transcendentals=0
        ),
    )(routes.T, event_weights.T, tokens, cotangent, w_gate, w_up, w_down)
    mixed, token_grad, weight_grad = pl.pallas_call(
        hand_over,
        out_shape=tuple(jax.ShapeDtypeStruct(x.shape, x.dtype) for x in results),
        in_specs=[full] * 3,
        out_specs=(full,) * 3,
        cost_estimate=pl.CostEstimate(flops=0, bytes_accessed=8 * rows * columns, transcendentals=0),
    )(*results)
    return mixed, token_grad, weight_grad.T


def fits(mesh, w_gate, routes):
    owners, splits, cores = mesh.shape["exp"], mesh.shape["ctx"], mesh.shape["rep"]
    experts, depth, hidden = w_gate.shape
    rows, fanout = routes.shape[0] // (owners * cores), routes.shape[1]
    capacity = max(2, 5 * rows * fanout // (4 * experts))
    columns = depth // splits
    return (
        experts == owners and 1 < owners <= 8 and splits > 1 and cores == 2 and fanout == 2
        and rows == 128 and capacity % 16 == 0 and columns % 128 == 0 and hidden % (128 * splits) == 0
        and 6 * columns * hidden <= 16 * 1024 * 1024
    )


def solution(mesh):
    in_specs = (
        P(("rep", "exp"), "ctx"),
        P(("rep", "exp"), None),
        P(("rep", "exp"), None),
        P("exp", "ctx"),
        P("exp", "ctx", None),
        P("exp", "ctx", None),
        P("exp", None, "ctx"),
    )
    out_specs = (P(("rep", "exp"), "ctx"), P(("rep", "exp"), "ctx"), P(("rep", "exp"), None))

    def run(tokens, routes, event_weights, cotangent, w_gate, w_up, w_down):
        body = shards_fused if fits(mesh, w_gate, routes) else shards
        mapped = jax.shard_map(body, mesh=mesh, in_specs=in_specs, out_specs=out_specs, check_vma=False)
        return mapped(tokens, routes, event_weights, cotangent, w_gate, w_up, w_down)

    return run
```

```python
import functools

import jax
import jax.numpy as jnp
from jax import lax
from jax.experimental import pallas as pl
from jax.experimental.pallas import tpu as pltpu
from jax.sharding import PartitionSpec as P


def activate(gate_pre, up_pre, back_pre):
    squash = jax.nn.sigmoid(gate_pre)
    hidden_act = (gate_pre * squash * up_pre).astype(jnp.bfloat16)
    grad_gate = (back_pre * up_pre * squash * (1.0 + gate_pre * (1.0 - squash))).astype(
        jnp.bfloat16
    )
    grad_up = (back_pre * gate_pre * squash).astype(jnp.bfloat16)
    return (hidden_act, grad_gate, grad_up)


def shards(tokens, routes, event_weights, cotangent, w_gate, w_up, w_down):
    owners = lax.axis_size("exp")
    owned, columns, hidden = w_gate.shape
    experts = owned * owners
    rows_here, fanout = routes.shape
    capacity = max(2, 5 * rows_here * fanout // (4 * experts))
    slot_count = owners * capacity
    routes_flat = routes.reshape(-1)
    onehot = (routes_flat[:, None] == jnp.arange(experts, dtype=jnp.int32)[None, :]).astype(
        jnp.int32
    )
    places = jnp.sum((jnp.cumsum(onehot, axis=0) - onehot) * onehot, axis=1)
    targets = routes_flat * capacity + places
    token_rows = jnp.repeat(tokens, fanout, axis=0)
    cot_rows = (
        event_weights.reshape(-1, 1) * jnp.repeat(cotangent.astype(jnp.float32), fanout, axis=0)
    ).astype(jnp.bfloat16)
    send_tokens = jnp.zeros((experts * capacity, columns), jnp.bfloat16).at[targets].set(token_rows)
    send_cots = jnp.zeros((experts * capacity, columns), jnp.bfloat16).at[targets].set(cot_rows)
    send_tokens = send_tokens.reshape(owners, owned * capacity, columns)
    send_cots = send_cots.reshape(owners, owned * capacity, columns)
    recv_tokens, recv_cots = (
        lax.all_to_all(send_tokens, "exp", split_axis=0, concat_axis=0, tiled=True),
        lax.all_to_all(send_cots, "exp", split_axis=0, concat_axis=0, tiled=True),
    )

    def arrange(buffer):
        return (
            buffer.reshape(owners, owned, capacity, columns)
            .transpose(1, 0, 2, 3)
            .reshape(owned, slot_count, columns)
        )

    expert_in = arrange(recv_tokens)
    expert_cot = arrange(recv_cots)
    shares = lax.psum_scatter(
        jnp.stack(
            [
                jnp.einsum("jsd,jdf->fjs", expert_in, w_gate, preferred_element_type=jnp.float32),
                jnp.einsum("jsd,jdf->fjs", expert_in, w_up, preferred_element_type=jnp.float32),
                jnp.einsum("jsd,jfd->fjs", expert_cot, w_down, preferred_element_type=jnp.float32),
            ],
            axis=1,
        ).astype(jnp.bfloat16),
        "ctx",
        scatter_dimension=0,
        tiled=True,
    ).astype(jnp.float32)
    hidden_share, gate_share, up_share = activate(shares[:, 0], shares[:, 1], shares[:, 2])
    hidden_act, grad_gate, grad_up = (
        lax.all_gather(hidden_share, "ctx", axis=0, tiled=True),
        lax.all_gather(gate_share, "ctx", axis=0, tiled=True),
        lax.all_gather(up_share, "ctx", axis=0, tiled=True),
    )
    expert_out = jnp.einsum(
        "fjs,jfd->jsd", hidden_act, w_down, preferred_element_type=jnp.float32
    ).astype(jnp.bfloat16)
    event_grad = (
        jnp.einsum("fjs,jdf->jsd", grad_gate, w_gate, preferred_element_type=jnp.float32)
        + jnp.einsum("fjs,jdf->jsd", grad_up, w_up, preferred_element_type=jnp.float32)
    ).astype(jnp.bfloat16)

    def restore(buffer):
        return (
            buffer.reshape(owned, owners, capacity, columns)
            .transpose(1, 0, 2, 3)
            .reshape(owners, owned * capacity, columns)
        )

    back_out, back_grad = (
        lax.all_to_all(restore(expert_out), "exp", split_axis=0, concat_axis=0, tiled=True),
        lax.all_to_all(restore(event_grad), "exp", split_axis=0, concat_axis=0, tiled=True),
    )
    out_rows = (
        back_out.reshape(experts * capacity, columns)[targets]
        .reshape(rows_here, fanout, columns)
        .astype(jnp.float32)
    )
    grad_rows = (
        back_grad.reshape(experts * capacity, columns)[targets]
        .reshape(rows_here, fanout, columns)
        .astype(jnp.float32)
    )
    mixed = jnp.sum(event_weights[:, :, None] * out_rows, axis=1).astype(jnp.bfloat16)
    token_grad = jnp.sum(grad_rows, axis=1).astype(jnp.bfloat16)
    weight_part = jnp.einsum("td,tkd->tk", cotangent.astype(jnp.float32), out_rows)
    weight_grad = lax.psum(weight_part, "ctx")
    return (mixed, token_grad, weight_grad)


def fused(
    sizes,
    routes_ref, weights_ref, tokens_ref, cot_ref, gate_hbm, up_hbm, down_hbm,
    mixed_ref, grad_ref, wgrad_ref,
    gate_w, up_w, down_w, x_send, x_recv, rt_recv, cots, part, shares, acts, grads, saved,
    stack, sums, sum_recv, pair_picks, slot_w, wg_send, wg_recv, wg_parts,
    load_sem, x_ssem, x_rsem, rt_ssem, rt_rsem, far_up, far_down, far_rsem, sib_ssem, sib_rsem,
    rs_ssem, rs_rsem, bk_ssem, bk_rsem, ag_ssem, ag_rsem, gg_ssem, gg_rsem,
    pair_ssem, pair_rsem, sum_ssem, sum_rsem, wgz_ssem, wgz_rsem, wg_ssem, wg_rsem,
):
    owners, splits, capacity, rows, columns, hidden = sizes
    part_f = hidden // splits
    half = rows // 2
    z, c, r = lax.axis_index("exp"), lax.axis_index("ctx"), lax.axis_index("rep")
    bf, f32 = jnp.bfloat16, jnp.float32

    def expert_at(d):
        return lax.rem(z + d, owners)

    def source_at(d):
        return lax.rem(z - d + owners, owners)

    def peer_at(q):
        return lax.rem(c + q, splits)

    def from_peer(q):
        return lax.rem(c - q + splits, splits)

    def remote(src, dst, ssem, rsem, **where):
        return pltpu.make_async_remote_copy(
            src_ref=src, dst_ref=dst, send_sem=ssem, recv_sem=rsem,
            device_id=where, device_id_type=pl.DeviceIdType.MESH,
        )

    loads = [
        pltpu.make_async_copy(gate_hbm.at[0], gate_w, load_sem.at[0]),
        pltpu.make_async_copy(up_hbm.at[0], up_w, load_sem.at[1]),
        pltpu.make_async_copy(down_hbm.at[0], down_w, load_sem.at[2]),
    ]
    for load in loads:
        load.start()

    barrier = pltpu.get_barrier_semaphore()
    for d in range(1, owners):
        pl.semaphore_signal(barrier, inc=1, device_id={"exp": expert_at(d)}, device_id_type=pl.DeviceIdType.MESH)
    for q in range(1, splits):
        pl.semaphore_signal(barrier, inc=1, device_id={"ctx": peer_at(q)}, device_id_type=pl.DeviceIdType.MESH)
    pl.semaphore_signal(barrier, inc=1, device_id={"rep": 1 - r}, device_id_type=pl.DeviceIdType.MESH)

    routes = routes_ref[...]
    event_w = weights_ref[...]
    row_i = lax.broadcasted_iota(jnp.int32, (rows, rows), 0)
    col_i = lax.broadcasted_iota(jnp.int32, (rows, rows), 1)
    upper = (row_i < col_i).astype(f32).astype(bf)
    experts_i = lax.broadcasted_iota(jnp.int32, (16, rows), 0)
    rt_recv[0, 0:2] = routes.astype(f32)
    rt_recv[0, 2:4] = event_w
    rt_recv[0, 4:] = jnp.zeros((4, rows), f32)

    end = z // 2
    partner = z + 1 - 2 * lax.rem(z, 2)
    inner = (z == 1) | (z == 2)

    def line(i):
        other = (z, partner, 2 - end, 3 * (1 - end))[i]
        return other, lax.rem(z - other + owners, owners), lax.rem(other - z + owners, owners)

    def picks(d, expert):
        r0, r1 = rt_recv[d, 0:1], rt_recv[d, 1:2]
        experts_f = experts_i.astype(f32)
        named = ((experts_f == r0) | (experts_f == r1)).astype(f32)
        pos = jnp.dot(named.astype(bf), upper, preferred_element_type=f32)
        mine = experts_i == expert
        pos_e = jnp.sum(jnp.where(mine, pos, 0.0), axis=0, keepdims=True)
        has_e = jnp.sum(jnp.where(mine, named, 0.0), axis=0, keepdims=True)
        place = lax.broadcasted_iota(jnp.int32, (capacity, rows), 0).astype(f32)
        return (place == pos_e) & (has_e > 0.5)

    def as_bf(mask):
        return mask.astype(f32).astype(bf)

    pl.semaphore_wait(barrier, owners + splits - 1)

    steps = range(1, owners)

    def rt(i):
        other, _, d = line(i)
        return remote(rt_recv.at[0], rt_recv.at[d], rt_ssem.at[i], rt_rsem.at[d], exp=other)

    def send_x(i):
        other, _, d = line(i)
        return remote(x_send.at[i], x_recv.at[d], x_ssem.at[i], x_rsem.at[d], exp=other)

    def got_x(i):
        other, d, _ = line(i)
        remote(rt_recv.at[0], rt_recv.at[d], rt_ssem.at[i], rt_rsem.at[d], exp=other).wait_recv()
        remote(x_send.at[i], x_recv.at[d], x_ssem.at[i], x_rsem.at[d], exp=other).wait_recv()
        return d

    for i in steps:
        rt(i).start()
    for i in steps:
        x_send[i] = jnp.dot(as_bf(picks(0, line(i)[0])), tokens_ref[...], preferred_element_type=f32).astype(bf)
        send_x(i).start()

    my_half = pl.ds(pl.multiple_of(r * half, half), half)

    def far(src, j, going_up):
        sem = far_up if going_up else far_down
        return remote(src, cots.at[j, my_half], sem.at[j], far_rsem.at[j], exp=z + (1 if going_up else -1))

    def sibling(j):
        return remote(cots.at[j, my_half], cots.at[j, my_half], sib_ssem.at[j], sib_rsem.at[j], rep=1 - r)

    @pl.when(z < owners - 1)
    def _():
        far(cot_ref.at[my_half], z, True).start()

    @pl.when(z > 0)
    def _():
        far(cot_ref.at[my_half], z, False).start()

    cots[z] = cot_ref[...]
    x_recv[0] = jnp.dot(as_bf(picks(0, z)), tokens_ref[...], preferred_element_type=f32).astype(bf)

    def pass_on(d):
        @pl.when(z - d >= 0)
        def _():
            j = z - d
            far(cots.at[j, my_half], j, True).wait_recv()

            @pl.when(z < owners - 1)
            def _():
                far(cots.at[j, my_half], j, True).start()

            sibling(j).start()

        @pl.when(z + d < owners)
        def _():
            j = z + d
            far(cots.at[j, my_half], j, False).wait_recv()

            @pl.when(z > 0)
            def _():
                far(cots.at[j, my_half], j, False).start()

            sibling(j).start()

    for load in loads:
        load.wait()

    def slices(p):
        return slice(p * part_f, (p + 1) * part_f)

    def first(d):
        x = x_recv[d]
        for p in range(splits):
            part[d, p, 0:capacity] = jnp.dot(x, gate_w[:, slices(p)], preferred_element_type=f32).astype(bf)
            part[d, p, capacity:2 * capacity] = jnp.dot(x, up_w[:, slices(p)], preferred_element_type=f32).astype(bf)

    def back(i, d):
        pick = pair_picks[i, 0:capacity]
        rows_in = jnp.dot(pick, cots[source_at(d)], preferred_element_type=f32).astype(bf)
        for p in range(splits):
            part[d, p, 2 * capacity:3 * capacity] = lax.dot_general(
                rows_in, down_w[slices(p), :], (((1,), (1,)), ((), ())), preferred_element_type=f32
            ).astype(bf)

    def rs(d, q):
        at = pl.ds(0, 2 * capacity)
        return remote(part.at[d, peer_at(q), at], shares.at[d, q, at], rs_ssem.at[d, q], rs_rsem.at[d, q], ctx=peer_at(q))

    def bk(d, q):
        at = pl.ds(2 * capacity, capacity)
        return remote(part.at[d, peer_at(q), at], shares.at[d, q, at], bk_ssem.at[d, q], bk_rsem.at[d, q], ctx=peer_at(q))

    def ag(d, q):
        return remote(acts.at[d, c], acts.at[d, c], ag_ssem.at[d, q], ag_rsem.at[d, q], ctx=peer_at(q))

    def gg(d, q):
        return remote(grads.at[d, c], grads.at[d, c], gg_ssem.at[d, q], gg_rsem.at[d, q], ctx=peer_at(q))

    own, landed = pl.ds(0, capacity), pl.ds(capacity, capacity)

    def to_partner(k, i):
        at = 0 if i == 1 else i
        return remote(stack.at[k, i, own], stack.at[k, at, landed], pair_ssem.at[k, i], pair_rsem.at[k, at], exp=partner)

    def landed_at(k, at):
        return remote(stack.at[k, at, own], stack.at[k, at, landed], pair_ssem.at[k, at], pair_rsem.at[k, at], exp=partner)

    def to_source(k, i):
        return remote(sums.at[k, i - 2], sum_recv.at[k], sum_ssem.at[k, i - 2], sum_rsem.at[k], exp=line(i)[0])

    def hand_on(k, i):
        if i == 1:
            to_partner(k, i).start()
        elif i > 1:
            @pl.when(~inner)
            def _():
                to_partner(k, i).start()

    step = 256 if columns % 256 == 0 else columns

    def relay(k, i):
        @pl.when(inner)
        def _():
            landed_at(k, i).wait_recv()
            for n in range(0, columns, step):
                sums[k, i - 2, :, n:n + step] = lax.dot_general(
                    pair_picks[i], stack[k, i, :, n:n + step], (((0,), (0,)), ((), ())), preferred_element_type=f32
                ).astype(bf)
            to_source(k, i).start()

    def wgz(i):
        other, d, _ = line(i)
        return remote(wg_send.at[i], wg_recv.at[d], wgz_ssem.at[i], wgz_rsem.at[d], exp=other)

    others = range(1, splits)

    def activate_block(d):
        for q in others:
            rs(d, q).wait_recv()
        both = part[d, c, 0:2 * capacity].astype(f32)
        for q in others:
            both = both + shares[d, q, 0:2 * capacity].astype(f32)
        saved[d] = both
        gate_pre, up_pre = both[0:capacity], both[capacity:]
        acts[d, c] = (gate_pre * jax.nn.sigmoid(gate_pre) * up_pre).astype(bf)
        for q in others:
            ag(d, q).start()

    def back_block(i):
        d = 0
        if i > 0:
            other, d, _ = line(i)
            sibling(other).wait_recv()
        back(i, d)
        for q in others:
            bk(d, q).start()

    def first_block(i):
        d = got_x(i) if i else 0
        first(d)
        mine = picks(d, z)
        pair_picks[i, 0:capacity] = as_bf(mine)
        if i != 1:
            pair_picks[i, capacity:] = as_bf(picks(d, partner))
        expert = z.astype(f32)
        named = jnp.where(rt_recv[d, 0:2] == expert, rt_recv[d, 2:4], 0.0)
        slot_w[i] = jnp.sum(jnp.where(mine, jnp.sum(named, axis=0, keepdims=True), 0.0), axis=1, keepdims=True)
        for q in others:
            rs(d, q).start()

    def slot(i):
        return line(i)[1] if i else 0

    def out_block(i):
        d = slot(i)
        for q in others:
            ag(d, q).wait_recv()
        act = jnp.concatenate([acts[d, p] for p in range(splits)], axis=1)
        weight = slot_w[i]
        for n in range(0, columns, step):
            stack[0, i, 0:capacity, n:n + step] = (
                weight * jnp.dot(act, down_w[:, n:n + step], preferred_element_type=f32)
            ).astype(bf)
        hand_on(0, i)

    def grad_block(i):
        d = slot(i)
        for q in others:
            bk(d, q).wait_recv()
        back_pre = part[d, c, 2 * capacity:].astype(f32)
        for q in others:
            back_pre = back_pre + shares[d, q, 2 * capacity:].astype(f32)
        gate_pre, up_pre = saved[d, 0:capacity], saved[d, capacity:]
        squash = jax.nn.sigmoid(gate_pre)
        per_slot = jnp.sum(acts[d, c].astype(f32) * back_pre, axis=1, keepdims=True)
        per_token = jnp.sum(jnp.where(pair_picks[i, 0:capacity].astype(f32) > 0.5, per_slot, 0.0), axis=0, keepdims=True)
        where_to = wg_send if i else wg_recv
        where_to[i] = jnp.broadcast_to(per_token, (8, rows))
        if i:
            wgz(i).start()
        back_pre = slot_w[i] * back_pre
        grads[d, c, 0:capacity] = (back_pre * up_pre * squash * (1.0 + gate_pre * (1.0 - squash))).astype(bf)
        grads[d, c, capacity:] = (back_pre * gate_pre * squash).astype(bf)
        for q in others:
            gg(d, q).start()

    def eg_block(i):
        d = slot(i)
        for q in others:
            gg(d, q).wait_recv()
        gate_g = jnp.concatenate([grads[d, p, 0:capacity] for p in range(splits)], axis=1)
        up_g = jnp.concatenate([grads[d, p, capacity:] for p in range(splits)], axis=1)
        for n in range(0, columns, step):
            nt = (((1,), (1,)), ((), ()))
            stack[1, i, 0:capacity, n:n + step] = (
                lax.dot_general(gate_g, gate_w[n:n + step], nt, preferred_element_type=f32)
                + lax.dot_general(up_g, up_w[n:n + step], nt, preferred_element_type=f32)
            ).astype(bf)
        hand_on(1, i)

    first_block(0)
    back_block(0)
    for i in steps:
        first_block(i)
        activate_block(slot(i - 1))
        if i > 1:
            out_block(i - 1)
        if i < 3:
            pass_on(i)
    activate_block(slot(3))
    back_block(1)
    out_block(3)
    pass_on(3)
    back_block(2)
    back_block(3)
    relay(0, 2)
    grad_block(0)
    grad_block(1)
    relay(0, 3)
    grad_block(2)
    grad_block(3)
    eg_block(2)
    eg_block(3)
    eg_block(1)
    relay(1, 2)
    out_block(0)
    relay(1, 3)
    eg_block(0)

    def wg(q):
        return remote(wg_parts.at[0], wg_parts.at[q], wg_ssem.at[q], wg_rsem.at[q], ctx=peer_at(q))

    acc = jnp.zeros(routes.shape, f32)
    for i in range(owners):
        expert, _, d = line(i)
        if i:
            remote(wg_send.at[i], wg_recv.at[d], wgz_ssem.at[i], wgz_rsem.at[d], exp=expert).wait_recv()
        acc = acc + jnp.where(routes == expert, wg_recv[d if i else 0, 0:1], 0.0)
    wg_parts[0, 0:routes.shape[0]] = acc
    wg_parts[0, routes.shape[0]:] = jnp.zeros((8 - routes.shape[0], rows), f32)
    for q in others:
        wg(q).start()

    def collect(k, into):
        landed_at(k, 0).wait_recv()
        to_source(k, 2).wait_recv()
        for n in range(0, columns, step):
            at = slice(n, n + step)
            here = lax.dot_general(pair_picks[0], stack[k, 0, :, at], (((0,), (0,)), ((), ())), preferred_element_type=f32)
            into[:, at] = (here + sum_recv[k, :, at].astype(f32)).astype(bf)

    collect(0, mixed_ref)
    for q in others:
        wg(q).wait_recv()
        acc = acc + wg_parts[q, 0:routes.shape[0]]
    wgrad_ref[...] = acc
    collect(1, grad_ref)

    for i in steps:
        send_x(i).wait_send()
        rt(i).wait_send()
        wgz(i).wait_send()
    for k in range(2):
        to_partner(k, 1).wait_send()
        for i in (2, 3):
            @pl.when(inner)
            def _():
                to_source(k, i).wait_send()

            @pl.when(~inner)
            def _():
                to_partner(k, i).wait_send()
    for q in others:
        wg(q).wait_send()
        for d in range(owners):
            rs(d, q).wait_send()
            bk(d, q).wait_send()
            ag(d, q).wait_send()
            gg(d, q).wait_send()

    @pl.when(z < owners - 1)
    def _():
        far(cot_ref.at[my_half], z, True).wait_send()

    @pl.when(z > 0)
    def _():
        far(cot_ref.at[my_half], z, False).wait_send()

    for d in range(1, owners):
        @pl.when(z - d >= 0)
        def _():
            @pl.when(z < owners - 1)
            def _():
                far(cots.at[z - d, my_half], z - d, True).wait_send()

            sibling(z - d).wait_send()

        @pl.when(z + d < owners)
        def _():
            @pl.when(z > 0)
            def _():
                far(cots.at[z + d, my_half], z + d, False).wait_send()

            sibling(z + d).wait_send()


def hand_over(*refs):
    for source, target in zip(refs[:3], refs[3:]):
        target[...] = source[...]


def shards_fused(tokens, routes, event_weights, cotangent, w_gate, w_up, w_down):
    owners, splits = lax.axis_size("exp"), lax.axis_size("ctx")
    _, columns, hidden = w_gate.shape
    rows, fanout = routes.shape
    capacity = max(2, 5 * rows * fanout // (4 * owners))
    part_f = hidden // splits
    sizes = (owners, splits, capacity, rows, columns, hidden)
    bf, f32 = jnp.bfloat16, jnp.float32
    vmem, dma = pltpu.VMEM, pltpu.SemaphoreType.DMA
    full = pl.BlockSpec(memory_space=pltpu.VMEM)
    anywhere = pl.BlockSpec(memory_space=pl.ANY)
    per_block = dma((owners,))
    per_pair = dma((owners, splits))
    moved = owners * capacity * columns
    results = pl.pallas_call(
        functools.partial(fused, sizes),
        out_shape=(
            jax.ShapeDtypeStruct((rows, columns), bf),
            jax.ShapeDtypeStruct((rows, columns), bf),
            jax.ShapeDtypeStruct((fanout, rows), f32),
        ),
        in_specs=[full, full, full, full, anywhere, anywhere, anywhere],
        out_specs=(full, full, full),
        scratch_shapes=[
            vmem((columns, hidden), bf), vmem((columns, hidden), bf), vmem((hidden, columns), bf),
            vmem((owners, capacity, columns), bf), vmem((owners, capacity, columns), bf),
            vmem((owners, 8, rows), f32),
            vmem((owners, rows, columns), bf),
            vmem((owners, splits, 3 * capacity, part_f), bf),
            vmem((owners, splits, 3 * capacity, part_f), bf),
            vmem((owners, splits, capacity, part_f), bf),
            vmem((owners, splits, 2 * capacity, part_f), bf),
            vmem((owners, 2 * capacity, part_f), f32),
            vmem((2, owners, 2 * capacity, columns), bf),
            vmem((2, 2, rows, columns), bf), vmem((2, rows, columns), bf),
            vmem((owners, 2 * capacity, rows), bf), vmem((owners, capacity, 1), f32),
            vmem((owners, 8, rows), f32), vmem((owners, 8, rows), f32), vmem((splits, 8, rows), f32),
            dma((3,)), per_block, per_block, per_block, per_block,
            per_block, per_block, per_block, per_block, per_block,
            per_pair, per_pair, per_pair, per_pair, per_pair, per_pair, per_pair, per_pair,
            dma((2, owners)), dma((2, owners)), dma((2, 2)), dma((2,)), per_block, per_block, dma((splits,)), dma((splits,)),
        ],
        compiler_params=pltpu.CompilerParams(
            collective_id=0, has_side_effects=True, vmem_limit_bytes=56 * 1024 * 1024
        ),
        cost_estimate=pl.CostEstimate(
            flops=12 * moved * hidden, bytes_accessed=6 * columns * hidden, transcendentals=0
        ),
    )(routes.T, event_weights.T, tokens, cotangent, w_gate, w_up, w_down)
    mixed, token_grad, weight_grad = pl.pallas_call(
        hand_over,
        out_shape=tuple(jax.ShapeDtypeStruct(x.shape, x.dtype) for x in results),
        in_specs=[full] * 3,
        out_specs=(full,) * 3,
        cost_estimate=pl.CostEstimate(flops=0, bytes_accessed=8 * rows * columns, transcendentals=0),
    )(*results)
    return mixed, token_grad, weight_grad.T


def fits(mesh, w_gate, routes):
    owners, splits, cores = mesh.shape["exp"], mesh.shape["ctx"], mesh.shape["rep"]
    experts, depth, hidden = w_gate.shape
    rows, fanout = routes.shape[0] // (owners * cores), routes.shape[1]
    capacity = max(2, 5 * rows * fanout // (4 * experts))
    columns = depth // splits
    return (
        experts == owners and owners == 4 and splits > 1 and cores == 2 and fanout == 2
        and rows == 128 and capacity % 16 == 0 and columns % 128 == 0 and hidden % (128 * splits) == 0
        and 6 * columns * hidden <= 16 * 1024 * 1024
    )


def solution(mesh):
    in_specs = (
        P(("rep", "exp"), "ctx"),
        P(("rep", "exp"), None),
        P(("rep", "exp"), None),
        P("exp", "ctx"),
        P("exp", "ctx", None),
        P("exp", "ctx", None),
        P("exp", None, "ctx"),
    )
    out_specs = (P(("rep", "exp"), "ctx"), P(("rep", "exp"), "ctx"), P(("rep", "exp"), None))

    def run(tokens, routes, event_weights, cotangent, w_gate, w_up, w_down):
        body = shards_fused if fits(mesh, w_gate, routes) else shards
        mapped = jax.shard_map(body, mesh=mesh, in_specs=in_specs, out_specs=out_specs, check_vma=False)
        return mapped(tokens, routes, event_weights, cotangent, w_gate, w_up, w_down)

    return run
```

```python
import functools

import jax
import jax.numpy as jnp
from jax import lax
from jax.experimental import pallas as pl
from jax.experimental.pallas import tpu as pltpu
from jax.sharding import PartitionSpec as P


def activate(gate_pre, up_pre, back_pre):
    squash = jax.nn.sigmoid(gate_pre)
    hidden_act = (gate_pre * squash * up_pre).astype(jnp.bfloat16)
    grad_gate = (back_pre * up_pre * squash * (1.0 + gate_pre * (1.0 - squash))).astype(
        jnp.bfloat16
    )
    grad_up = (back_pre * gate_pre * squash).astype(jnp.bfloat16)
    return (hidden_act, grad_gate, grad_up)


def shards(tokens, routes, event_weights, cotangent, w_gate, w_up, w_down):
    owners = lax.axis_size("exp")
    owned, columns, hidden = w_gate.shape
    experts = owned * owners
    rows_here, fanout = routes.shape
    capacity = max(2, 5 * rows_here * fanout // (4 * experts))
    slot_count = owners * capacity
    routes_flat = routes.reshape(-1)
    onehot = (routes_flat[:, None] == jnp.arange(experts, dtype=jnp.int32)[None, :]).astype(
        jnp.int32
    )
    places = jnp.sum((jnp.cumsum(onehot, axis=0) - onehot) * onehot, axis=1)
    targets = routes_flat * capacity + places
    token_rows = jnp.repeat(tokens, fanout, axis=0)
    cot_rows = (
        event_weights.reshape(-1, 1) * jnp.repeat(cotangent.astype(jnp.float32), fanout, axis=0)
    ).astype(jnp.bfloat16)
    send_tokens = jnp.zeros((experts * capacity, columns), jnp.bfloat16).at[targets].set(token_rows)
    send_cots = jnp.zeros((experts * capacity, columns), jnp.bfloat16).at[targets].set(cot_rows)
    send_tokens = send_tokens.reshape(owners, owned * capacity, columns)
    send_cots = send_cots.reshape(owners, owned * capacity, columns)
    recv_tokens, recv_cots = (
        lax.all_to_all(send_tokens, "exp", split_axis=0, concat_axis=0, tiled=True),
        lax.all_to_all(send_cots, "exp", split_axis=0, concat_axis=0, tiled=True),
    )

    def arrange(buffer):
        return (
            buffer.reshape(owners, owned, capacity, columns)
            .transpose(1, 0, 2, 3)
            .reshape(owned, slot_count, columns)
        )

    expert_in = arrange(recv_tokens)
    expert_cot = arrange(recv_cots)
    shares = lax.psum_scatter(
        jnp.stack(
            [
                jnp.einsum("jsd,jdf->fjs", expert_in, w_gate, preferred_element_type=jnp.float32),
                jnp.einsum("jsd,jdf->fjs", expert_in, w_up, preferred_element_type=jnp.float32),
                jnp.einsum("jsd,jfd->fjs", expert_cot, w_down, preferred_element_type=jnp.float32),
            ],
            axis=1,
        ).astype(jnp.bfloat16),
        "ctx",
        scatter_dimension=0,
        tiled=True,
    ).astype(jnp.float32)
    hidden_share, gate_share, up_share = activate(shares[:, 0], shares[:, 1], shares[:, 2])
    hidden_act, grad_gate, grad_up = (
        lax.all_gather(hidden_share, "ctx", axis=0, tiled=True),
        lax.all_gather(gate_share, "ctx", axis=0, tiled=True),
        lax.all_gather(up_share, "ctx", axis=0, tiled=True),
    )
    expert_out = jnp.einsum(
        "fjs,jfd->jsd", hidden_act, w_down, preferred_element_type=jnp.float32
    ).astype(jnp.bfloat16)
    event_grad = (
        jnp.einsum("fjs,jdf->jsd", grad_gate, w_gate, preferred_element_type=jnp.float32)
        + jnp.einsum("fjs,jdf->jsd", grad_up, w_up, preferred_element_type=jnp.float32)
    ).astype(jnp.bfloat16)

    def restore(buffer):
        return (
            buffer.reshape(owned, owners, capacity, columns)
            .transpose(1, 0, 2, 3)
            .reshape(owners, owned * capacity, columns)
        )

    back_out, back_grad = (
        lax.all_to_all(restore(expert_out), "exp", split_axis=0, concat_axis=0, tiled=True),
        lax.all_to_all(restore(event_grad), "exp", split_axis=0, concat_axis=0, tiled=True),
    )
    out_rows = (
        back_out.reshape(experts * capacity, columns)[targets]
        .reshape(rows_here, fanout, columns)
        .astype(jnp.float32)
    )
    grad_rows = (
        back_grad.reshape(experts * capacity, columns)[targets]
        .reshape(rows_here, fanout, columns)
        .astype(jnp.float32)
    )
    mixed = jnp.sum(event_weights[:, :, None] * out_rows, axis=1).astype(jnp.bfloat16)
    token_grad = jnp.sum(grad_rows, axis=1).astype(jnp.bfloat16)
    weight_part = jnp.einsum("td,tkd->tk", cotangent.astype(jnp.float32), out_rows)
    weight_grad = lax.psum(weight_part, "ctx")
    return (mixed, token_grad, weight_grad)


def fused(
    sizes,
    routes_ref, weights_ref, tokens_ref, cot_ref, gate_hbm, up_hbm, down_hbm,
    mixed_ref, grad_ref, wgrad_ref,
    gate_w, up_w, down_w, x_send, x_recv, rt_recv, cots, part, shares, acts, grads, saved,
    stack, far_rows, sums, sum_recv, pair_picks, slot_w, wg_send, wg_recv, wg_parts,
    load_sem, x_ssem, x_rsem, rt_ssem, rt_rsem, far_up, far_down, far_rsem, sib_ssem, sib_rsem,
    rs_ssem, rs_rsem, bk_ssem, bk_rsem, ag_ssem, ag_rsem, gg_ssem, gg_rsem,
    pair_ssem, pair_rsem, direct_ssem, direct_rsem, sum_ssem, sum_rsem, wgz_ssem, wgz_rsem, wg_ssem, wg_rsem,
):
    owners, splits, capacity, rows, columns, hidden = sizes
    part_f = hidden // splits
    half = rows // 2
    z, c, r = lax.axis_index("exp"), lax.axis_index("ctx"), lax.axis_index("rep")
    bf, f32 = jnp.bfloat16, jnp.float32

    def expert_at(d):
        return lax.rem(z + d, owners)

    def source_at(d):
        return lax.rem(z - d + owners, owners)

    def peer_at(q):
        return lax.rem(c + q, splits)

    def from_peer(q):
        return lax.rem(c - q + splits, splits)

    def remote(src, dst, ssem, rsem, **where):
        return pltpu.make_async_remote_copy(
            src_ref=src, dst_ref=dst, send_sem=ssem, recv_sem=rsem,
            device_id=where, device_id_type=pl.DeviceIdType.MESH,
        )

    loads = [
        pltpu.make_async_copy(gate_hbm.at[0], gate_w, load_sem.at[0]),
        pltpu.make_async_copy(up_hbm.at[0], up_w, load_sem.at[1]),
        pltpu.make_async_copy(down_hbm.at[0], down_w, load_sem.at[2]),
    ]
    for load in loads:
        load.start()

    barrier = pltpu.get_barrier_semaphore()
    for d in range(1, owners):
        pl.semaphore_signal(barrier, inc=1, device_id={"exp": expert_at(d)}, device_id_type=pl.DeviceIdType.MESH)
    for q in range(1, splits):
        pl.semaphore_signal(barrier, inc=1, device_id={"ctx": peer_at(q)}, device_id_type=pl.DeviceIdType.MESH)
    pl.semaphore_signal(barrier, inc=1, device_id={"rep": 1 - r}, device_id_type=pl.DeviceIdType.MESH)

    routes = routes_ref[...]
    event_w = weights_ref[...]
    row_i = lax.broadcasted_iota(jnp.int32, (rows, rows), 0)
    col_i = lax.broadcasted_iota(jnp.int32, (rows, rows), 1)
    upper = (row_i < col_i).astype(f32).astype(bf)
    experts_i = lax.broadcasted_iota(jnp.int32, (16, rows), 0)
    rt_recv[0, 0:2] = routes.astype(f32)
    rt_recv[0, 2:4] = event_w
    rt_recv[0, 4:] = jnp.zeros((4, rows), f32)

    end = z // 2
    partner = z + 1 - 2 * lax.rem(z, 2)
    inner = (z == 1) | (z == 2)

    def line(i):
        other = (z, partner, 2 - end, 3 * (1 - end))[i]
        return other, lax.rem(z - other + owners, owners), lax.rem(other - z + owners, owners)

    def picks(d, expert):
        r0, r1 = rt_recv[d, 0:1], rt_recv[d, 1:2]
        experts_f = experts_i.astype(f32)
        named = ((experts_f == r0) | (experts_f == r1)).astype(f32)
        pos = jnp.dot(named.astype(bf), upper, preferred_element_type=f32)
        mine = experts_i == expert
        pos_e = jnp.sum(jnp.where(mine, pos, 0.0), axis=0, keepdims=True)
        has_e = jnp.sum(jnp.where(mine, named, 0.0), axis=0, keepdims=True)
        place = lax.broadcasted_iota(jnp.int32, (capacity, rows), 0).astype(f32)
        return (place == pos_e) & (has_e > 0.5)

    def slot(i):
        return line(i)[1] if i else 0

    def as_bf(mask):
        return mask.astype(f32).astype(bf)

    pl.semaphore_wait(barrier, owners + splits - 1)

    steps = range(1, owners)

    def rt(i):
        other, _, d = line(i)
        return remote(rt_recv.at[0], rt_recv.at[d], rt_ssem.at[i], rt_rsem.at[d], exp=other)

    def send_x(i):
        other, _, d = line(i)
        return remote(x_send.at[i], x_recv.at[d], x_ssem.at[i], x_rsem.at[d], exp=other)

    def got_x(i):
        other, d, _ = line(i)
        remote(rt_recv.at[0], rt_recv.at[d], rt_ssem.at[i], rt_rsem.at[d], exp=other).wait_recv()
        remote(x_send.at[i], x_recv.at[d], x_ssem.at[i], x_rsem.at[d], exp=other).wait_recv()
        return d

    for i in steps:
        rt(i).start()
    for i in steps:
        x_send[i] = jnp.dot(as_bf(picks(0, line(i)[0])), tokens_ref[...], preferred_element_type=f32).astype(bf)
        send_x(i).start()

    my_half = pl.ds(pl.multiple_of(r * half, half), half)

    def far(src, j, going_up):
        sem = far_up if going_up else far_down
        return remote(src, cots.at[j, my_half], sem.at[j], far_rsem.at[j], exp=z + (1 if going_up else -1))

    def sibling(j):
        return remote(cots.at[j, my_half], cots.at[j, my_half], sib_ssem.at[j], sib_rsem.at[j], rep=1 - r)

    def start_cots():
        @pl.when(z < owners - 1)
        def _():
            far(cot_ref.at[my_half], z, True).start()

        @pl.when(z > 0)
        def _():
            far(cot_ref.at[my_half], z, False).start()

    cots[z] = cot_ref[...]
    x_recv[0] = jnp.dot(as_bf(picks(0, z)), tokens_ref[...], preferred_element_type=f32).astype(bf)

    def pass_on(d):
        @pl.when(z - d >= 0)
        def _():
            j = z - d
            far(cots.at[j, my_half], j, True).wait_recv()

            @pl.when(z < owners - 1)
            def _():
                far(cots.at[j, my_half], j, True).start()

            sibling(j).start()

        @pl.when(z + d < owners)
        def _():
            j = z + d
            far(cots.at[j, my_half], j, False).wait_recv()

            @pl.when(z > 0)
            def _():
                far(cots.at[j, my_half], j, False).start()

            sibling(j).start()

    for load in loads:
        load.wait()

    def slices(p):
        return slice(p * part_f, (p + 1) * part_f)

    def first(pair):
        x = jnp.concatenate([x_recv[slot(i)] for i in pair], axis=0)
        for p in range(splits):
            gate = jnp.dot(x, gate_w[:, slices(p)], preferred_element_type=f32).astype(bf)
            up = jnp.dot(x, up_w[:, slices(p)], preferred_element_type=f32).astype(bf)
            for n, i in enumerate(pair):
                part[slot(i), p, 0:capacity] = gate[n * capacity:(n + 1) * capacity]
                part[slot(i), p, capacity:2 * capacity] = up[n * capacity:(n + 1) * capacity]

    def back(pair):
        rows_in = jnp.concatenate([
            jnp.dot(pair_picks[i, 0:capacity], cots[source_at(slot(i))], preferred_element_type=f32).astype(bf)
            for i in pair
        ], axis=0)
        for p in range(splits):
            got = lax.dot_general(
                rows_in, down_w[slices(p), :], (((1,), (1,)), ((), ())), preferred_element_type=f32
            ).astype(bf)
            for n, i in enumerate(pair):
                part[slot(i), p, 2 * capacity:3 * capacity] = got[n * capacity:(n + 1) * capacity]

    def rs(d, q):
        at = pl.ds(0, 2 * capacity)
        return remote(part.at[d, peer_at(q), at], shares.at[d, q, at], rs_ssem.at[d, q], rs_rsem.at[d, q], ctx=peer_at(q))

    def bk(d, q):
        at = pl.ds(2 * capacity, capacity)
        return remote(part.at[d, peer_at(q), at], shares.at[d, q, at], bk_ssem.at[d, q], bk_rsem.at[d, q], ctx=peer_at(q))

    def ag(d, q):
        return remote(acts.at[d, c], acts.at[d, c], ag_ssem.at[d, q], ag_rsem.at[d, q], ctx=peer_at(q))

    def gg(d, q):
        return remote(grads.at[d, c], grads.at[d, c], gg_ssem.at[d, q], gg_rsem.at[d, q], ctx=peer_at(q))

    own, landed = pl.ds(0, capacity), pl.ds(capacity, capacity)

    def to_partner(k, i):
        at = 0 if i == 1 else i
        return remote(stack.at[k, i, own], stack.at[k, at, landed], pair_ssem.at[k, i], pair_rsem.at[k, at], exp=partner)

    def landed_at(k, at):
        return remote(stack.at[k, at, own], stack.at[k, at, landed], pair_ssem.at[k, at], pair_rsem.at[k, at], exp=partner)

    def to_source(k, i):
        return remote(sums.at[k, i - 2], sum_recv.at[k], sum_ssem.at[k, i - 2], sum_rsem.at[k], exp=line(i)[0])

    def direct(i):
        at = pl.ds(pl.multiple_of(jnp.where(inner, 0, capacity), capacity), capacity)
        return remote(stack.at[0, i, own], far_rows.at[at], direct_ssem.at[i - 2], direct_rsem.at[jnp.where(inner, 0, 1)], exp=line(i)[0])

    def got_direct(n):
        at = pl.ds(n * capacity, capacity)
        return remote(stack.at[0, 2 + n, own], far_rows.at[at], direct_ssem.at[n], direct_rsem.at[n], exp=line(2 + n)[0])

    def hand_on(k, i):
        if i == 1:
            to_partner(k, i).start()
        elif i > 1 and k == 0:
            direct(i).start()
        elif i > 1:
            @pl.when(~inner)
            def _():
                to_partner(k, i).start()

    step = 256 if columns % 256 == 0 else columns

    def relay(k, i):
        @pl.when(inner)
        def _():
            landed_at(k, i).wait_recv()
            for n in range(0, columns, step):
                sums[k, i - 2, :, n:n + step] = lax.dot_general(
                    pair_picks[i], stack[k, i, :, n:n + step], (((0,), (0,)), ((), ())), preferred_element_type=f32
                ).astype(bf)
            to_source(k, i).start()

    def wgz(i):
        other, d, _ = line(i)
        return remote(wg_send.at[i], wg_recv.at[d], wgz_ssem.at[i], wgz_rsem.at[d], exp=other)

    others = range(1, splits)

    def activate_block(d):
        for q in others:
            rs(d, q).wait_recv()
        both = part[d, c, 0:2 * capacity].astype(f32)
        for q in others:
            both = both + shares[d, q, 0:2 * capacity].astype(f32)
        saved[d] = both
        gate_pre, up_pre = both[0:capacity], both[capacity:]
        acts[d, c] = (gate_pre * jax.nn.sigmoid(gate_pre) * up_pre).astype(bf)
        for q in others:
            ag(d, q).start()

    def back_blocks(pair):
        for i in pair:
            if i:
                sibling(line(i)[0]).wait_recv()
        back(pair)
        for i in pair:
            for q in others:
                bk(slot(i), q).start()

    def pick_block(i):
        d = slot(i)
        mine = picks(d, z)
        pair_picks[i, 0:capacity] = as_bf(mine)
        if i != 1:
            pair_picks[i, capacity:] = as_bf(picks(d, partner))
        expert = z.astype(f32)
        weights = jnp.where(rt_recv[d, 0:2] == expert, rt_recv[d, 2:4], 0.0)
        slot_w[i] = jnp.sum(jnp.where(mine, jnp.sum(weights, axis=0, keepdims=True), 0.0), axis=1, keepdims=True)

    def first_blocks(pair):
        first(pair)
        for i in pair:
            for q in others:
                rs(slot(i), q).start()
        for i in pair:
            pick_block(i)

    def out_blocks(pair):
        for i in pair:
            for q in others:
                ag(slot(i), q).wait_recv()
        act = jnp.concatenate([
            jnp.concatenate([acts[slot(i), p] for p in range(splits)], axis=1) for i in pair
        ], axis=0)
        for n in range(0, columns, step):
            got = jnp.dot(act, down_w[:, n:n + step], preferred_element_type=f32)
            for m, i in enumerate(pair):
                stack[0, i, 0:capacity, n:n + step] = (slot_w[i] * got[m * capacity:(m + 1) * capacity]).astype(bf)
        for i in pair:
            hand_on(0, i)

    def grad_block(i):
        d = slot(i)
        for q in others:
            bk(d, q).wait_recv()
        back_pre = part[d, c, 2 * capacity:].astype(f32)
        for q in others:
            back_pre = back_pre + shares[d, q, 2 * capacity:].astype(f32)
        gate_pre, up_pre = saved[d, 0:capacity], saved[d, capacity:]
        squash = jax.nn.sigmoid(gate_pre)
        per_slot = jnp.sum(acts[d, c].astype(f32) * back_pre, axis=1, keepdims=True)
        per_token = jnp.sum(jnp.where(pair_picks[i, 0:capacity].astype(f32) > 0.5, per_slot, 0.0), axis=0, keepdims=True)
        where_to = wg_send if i else wg_recv
        where_to[i] = jnp.broadcast_to(per_token, (8, rows))
        if i:
            wgz(i).start()
        back_pre = slot_w[i] * back_pre
        grads[d, c, 0:capacity] = (back_pre * up_pre * squash * (1.0 + gate_pre * (1.0 - squash))).astype(bf)
        grads[d, c, capacity:] = (back_pre * gate_pre * squash).astype(bf)
        for q in others:
            gg(d, q).start()

    def eg_blocks(pair):
        for i in pair:
            for q in others:
                gg(slot(i), q).wait_recv()
        gate_g = jnp.concatenate([
            jnp.concatenate([grads[slot(i), p, 0:capacity] for p in range(splits)], axis=1) for i in pair
        ], axis=0)
        up_g = jnp.concatenate([
            jnp.concatenate([grads[slot(i), p, capacity:] for p in range(splits)], axis=1) for i in pair
        ], axis=0)
        nt = (((1,), (1,)), ((), ()))
        for n in range(0, columns, step):
            got = (
                lax.dot_general(gate_g, gate_w[n:n + step], nt, preferred_element_type=f32)
                + lax.dot_general(up_g, up_w[n:n + step], nt, preferred_element_type=f32)
            ).astype(bf)
            for m, i in enumerate(pair):
                stack[1, i, 0:capacity, n:n + step] = got[m * capacity:(m + 1) * capacity]
        for i in pair:
            hand_on(1, i)

    near, distant = (0, 1), (2, 3)
    got_x(1)
    first_blocks(near)
    activate_block(slot(0))
    activate_block(slot(1))
    got_x(2)
    start_cots()
    got_x(3)
    first_blocks(distant)
    out_blocks(near)
    pass_on(1)
    activate_block(slot(2))
    activate_block(slot(3))
    back_blocks(near)
    out_blocks(distant)
    pass_on(2)
    pass_on(3)
    back_blocks(distant)
    for i in range(owners):
        grad_block(i)
    eg_blocks(distant)
    eg_blocks(near)
    relay(1, 2)
    relay(1, 3)

    def wg(q):
        return remote(wg_parts.at[0], wg_parts.at[q], wg_ssem.at[q], wg_rsem.at[q], ctx=peer_at(q))

    acc = jnp.zeros(routes.shape, f32)
    for i in range(owners):
        expert, _, d = line(i)
        if i:
            remote(wg_send.at[i], wg_recv.at[d], wgz_ssem.at[i], wgz_rsem.at[d], exp=expert).wait_recv()
        acc = acc + jnp.where(routes == expert, wg_recv[d if i else 0, 0:1], 0.0)
    wg_parts[0, 0:routes.shape[0]] = acc
    wg_parts[0, routes.shape[0]:] = jnp.zeros((8 - routes.shape[0], rows), f32)
    for q in others:
        wg(q).start()

    tn = (((0,), (0,)), ((), ()))
    far_picks = jnp.concatenate([as_bf(picks(0, line(2)[0])), as_bf(picks(0, line(3)[0]))], axis=0)
    landed_at(0, 0).wait_recv()
    got_direct(0).wait_recv()
    got_direct(1).wait_recv()
    for n in range(0, columns, step):
        at = slice(n, n + step)
        mixed_ref[:, at] = (
            lax.dot_general(pair_picks[0], stack[0, 0, :, at], tn, preferred_element_type=f32)
            + lax.dot_general(far_picks, far_rows[:, at], tn, preferred_element_type=f32)
        ).astype(bf)
    for q in others:
        wg(q).wait_recv()
        acc = acc + wg_parts[q, 0:routes.shape[0]]
    wgrad_ref[...] = acc
    landed_at(1, 0).wait_recv()
    to_source(1, 2).wait_recv()
    for n in range(0, columns, step):
        at = slice(n, n + step)
        here = lax.dot_general(pair_picks[0], stack[1, 0, :, at], tn, preferred_element_type=f32)
        grad_ref[:, at] = (here + sum_recv[1, :, at].astype(f32)).astype(bf)

    for i in steps:
        send_x(i).wait_send()
        rt(i).wait_send()
        wgz(i).wait_send()
    to_partner(0, 1).wait_send()
    to_partner(1, 1).wait_send()
    for i in (2, 3):
        direct(i).wait_send()

        @pl.when(inner)
        def _():
            to_source(1, i).wait_send()

        @pl.when(~inner)
        def _():
            to_partner(1, i).wait_send()
    for q in others:
        wg(q).wait_send()
        for d in range(owners):
            rs(d, q).wait_send()
            bk(d, q).wait_send()
            ag(d, q).wait_send()
            gg(d, q).wait_send()

    @pl.when(z < owners - 1)
    def _():
        far(cot_ref.at[my_half], z, True).wait_send()

    @pl.when(z > 0)
    def _():
        far(cot_ref.at[my_half], z, False).wait_send()

    for d in range(1, owners):
        @pl.when(z - d >= 0)
        def _():
            @pl.when(z < owners - 1)
            def _():
                far(cots.at[z - d, my_half], z - d, True).wait_send()

            sibling(z - d).wait_send()

        @pl.when(z + d < owners)
        def _():
            @pl.when(z > 0)
            def _():
                far(cots.at[z + d, my_half], z + d, False).wait_send()

            sibling(z + d).wait_send()


def hand_over(*refs):
    for source, target in zip(refs[:3], refs[3:]):
        target[...] = source[...]


def shards_fused(tokens, routes, event_weights, cotangent, w_gate, w_up, w_down):
    owners, splits = lax.axis_size("exp"), lax.axis_size("ctx")
    _, columns, hidden = w_gate.shape
    rows, fanout = routes.shape
    capacity = max(2, 5 * rows * fanout // (4 * owners))
    part_f = hidden // splits
    sizes = (owners, splits, capacity, rows, columns, hidden)
    bf, f32 = jnp.bfloat16, jnp.float32
    vmem, dma = pltpu.VMEM, pltpu.SemaphoreType.DMA
    full = pl.BlockSpec(memory_space=pltpu.VMEM)
    anywhere = pl.BlockSpec(memory_space=pl.ANY)
    per_block = dma((owners,))
    per_pair = dma((owners, splits))
    moved = owners * capacity * columns
    results = pl.pallas_call(
        functools.partial(fused, sizes),
        out_shape=(
            jax.ShapeDtypeStruct((rows, columns), bf),
            jax.ShapeDtypeStruct((rows, columns), bf),
            jax.ShapeDtypeStruct((fanout, rows), f32),
        ),
        in_specs=[full, full, full, full, anywhere, anywhere, anywhere],
        out_specs=(full, full, full),
        scratch_shapes=[
            vmem((columns, hidden), bf), vmem((columns, hidden), bf), vmem((hidden, columns), bf),
            vmem((owners, capacity, columns), bf), vmem((owners, capacity, columns), bf),
            vmem((owners, 8, rows), f32),
            vmem((owners, rows, columns), bf),
            vmem((owners, splits, 3 * capacity, part_f), bf),
            vmem((owners, splits, 3 * capacity, part_f), bf),
            vmem((owners, splits, capacity, part_f), bf),
            vmem((owners, splits, 2 * capacity, part_f), bf),
            vmem((owners, 2 * capacity, part_f), f32),
            vmem((2, owners, 2 * capacity, columns), bf),
            vmem((2 * capacity, columns), bf), vmem((2, 2, rows, columns), bf), vmem((2, rows, columns), bf),
            vmem((owners, 2 * capacity, rows), bf), vmem((owners, capacity, 1), f32),
            vmem((owners, 8, rows), f32), vmem((owners, 8, rows), f32), vmem((splits, 8, rows), f32),
            dma((3,)), per_block, per_block, per_block, per_block,
            per_block, per_block, per_block, per_block, per_block,
            per_pair, per_pair, per_pair, per_pair, per_pair, per_pair, per_pair, per_pair,
            dma((2, owners)), dma((2, owners)), dma((2,)), dma((2,)), dma((2, 2)), dma((2,)), per_block, per_block, dma((splits,)), dma((splits,)),
        ],
        compiler_params=pltpu.CompilerParams(
            collective_id=0, has_side_effects=True, vmem_limit_bytes=56 * 1024 * 1024
        ),
        cost_estimate=pl.CostEstimate(
            flops=12 * moved * hidden, bytes_accessed=6 * columns * hidden, transcendentals=0
        ),
    )(routes.T, event_weights.T, tokens, cotangent, w_gate, w_up, w_down)
    mixed, token_grad, weight_grad = pl.pallas_call(
        hand_over,
        out_shape=tuple(jax.ShapeDtypeStruct(x.shape, x.dtype) for x in results),
        in_specs=[full] * 3,
        out_specs=(full,) * 3,
        cost_estimate=pl.CostEstimate(flops=0, bytes_accessed=8 * rows * columns, transcendentals=0),
    )(*results)
    return mixed, token_grad, weight_grad.T


def fits(mesh, w_gate, routes):
    owners, splits, cores = mesh.shape["exp"], mesh.shape["ctx"], mesh.shape["rep"]
    experts, depth, hidden = w_gate.shape
    rows, fanout = routes.shape[0] // (owners * cores), routes.shape[1]
    capacity = max(2, 5 * rows * fanout // (4 * experts))
    columns = depth // splits
    return (
        experts == owners and owners == 4 and splits > 1 and cores == 2 and fanout == 2
        and rows == 128 and capacity % 16 == 0 and columns % 128 == 0 and hidden % (128 * splits) == 0
        and 6 * columns * hidden <= 16 * 1024 * 1024
    )


def solution(mesh):
    in_specs = (
        P(("rep", "exp"), "ctx"),
        P(("rep", "exp"), None),
        P(("rep", "exp"), None),
        P("exp", "ctx"),
        P("exp", "ctx", None),
        P("exp", "ctx", None),
        P("exp", None, "ctx"),
    )
    out_specs = (P(("rep", "exp"), "ctx"), P(("rep", "exp"), "ctx"), P(("rep", "exp"), None))

    def run(tokens, routes, event_weights, cotangent, w_gate, w_up, w_down):
        body = shards_fused if fits(mesh, w_gate, routes) else shards
        mapped = jax.shard_map(body, mesh=mesh, in_specs=in_specs, out_specs=out_specs, check_vma=False)
        return mapped(tokens, routes, event_weights, cotangent, w_gate, w_up, w_down)

    return run
```

```python
import functools

import jax
import jax.numpy as jnp
from jax import lax
from jax.experimental import pallas as pl
from jax.experimental.pallas import tpu as pltpu
from jax.sharding import PartitionSpec as P


def activate(gate_pre, up_pre, back_pre):
    squash = jax.nn.sigmoid(gate_pre)
    hidden_act = (gate_pre * squash * up_pre).astype(jnp.bfloat16)
    grad_gate = (back_pre * up_pre * squash * (1.0 + gate_pre * (1.0 - squash))).astype(
        jnp.bfloat16
    )
    grad_up = (back_pre * gate_pre * squash).astype(jnp.bfloat16)
    return (hidden_act, grad_gate, grad_up)


def shards(tokens, routes, event_weights, cotangent, w_gate, w_up, w_down):
    owners = lax.axis_size("exp")
    owned, columns, hidden = w_gate.shape
    experts = owned * owners
    rows_here, fanout = routes.shape
    capacity = max(2, 5 * rows_here * fanout // (4 * experts))
    slot_count = owners * capacity
    routes_flat = routes.reshape(-1)
    onehot = (routes_flat[:, None] == jnp.arange(experts, dtype=jnp.int32)[None, :]).astype(
        jnp.int32
    )
    places = jnp.sum((jnp.cumsum(onehot, axis=0) - onehot) * onehot, axis=1)
    targets = routes_flat * capacity + places
    token_rows = jnp.repeat(tokens, fanout, axis=0)
    cot_rows = (
        event_weights.reshape(-1, 1) * jnp.repeat(cotangent.astype(jnp.float32), fanout, axis=0)
    ).astype(jnp.bfloat16)
    send_tokens = jnp.zeros((experts * capacity, columns), jnp.bfloat16).at[targets].set(token_rows)
    send_cots = jnp.zeros((experts * capacity, columns), jnp.bfloat16).at[targets].set(cot_rows)
    send_tokens = send_tokens.reshape(owners, owned * capacity, columns)
    send_cots = send_cots.reshape(owners, owned * capacity, columns)
    recv_tokens, recv_cots = (
        lax.all_to_all(send_tokens, "exp", split_axis=0, concat_axis=0, tiled=True),
        lax.all_to_all(send_cots, "exp", split_axis=0, concat_axis=0, tiled=True),
    )

    def arrange(buffer):
        return (
            buffer.reshape(owners, owned, capacity, columns)
            .transpose(1, 0, 2, 3)
            .reshape(owned, slot_count, columns)
        )

    expert_in = arrange(recv_tokens)
    expert_cot = arrange(recv_cots)
    shares = lax.psum_scatter(
        jnp.stack(
            [
                jnp.einsum("jsd,jdf->fjs", expert_in, w_gate, preferred_element_type=jnp.float32),
                jnp.einsum("jsd,jdf->fjs", expert_in, w_up, preferred_element_type=jnp.float32),
                jnp.einsum("jsd,jfd->fjs", expert_cot, w_down, preferred_element_type=jnp.float32),
            ],
            axis=1,
        ).astype(jnp.bfloat16),
        "ctx",
        scatter_dimension=0,
        tiled=True,
    ).astype(jnp.float32)
    hidden_share, gate_share, up_share = activate(shares[:, 0], shares[:, 1], shares[:, 2])
    hidden_act, grad_gate, grad_up = (
        lax.all_gather(hidden_share, "ctx", axis=0, tiled=True),
        lax.all_gather(gate_share, "ctx", axis=0, tiled=True),
        lax.all_gather(up_share, "ctx", axis=0, tiled=True),
    )
    expert_out = jnp.einsum(
        "fjs,jfd->jsd", hidden_act, w_down, preferred_element_type=jnp.float32
    ).astype(jnp.bfloat16)
    event_grad = (
        jnp.einsum("fjs,jdf->jsd", grad_gate, w_gate, preferred_element_type=jnp.float32)
        + jnp.einsum("fjs,jdf->jsd", grad_up, w_up, preferred_element_type=jnp.float32)
    ).astype(jnp.bfloat16)

    def restore(buffer):
        return (
            buffer.reshape(owned, owners, capacity, columns)
            .transpose(1, 0, 2, 3)
            .reshape(owners, owned * capacity, columns)
        )

    back_out, back_grad = (
        lax.all_to_all(restore(expert_out), "exp", split_axis=0, concat_axis=0, tiled=True),
        lax.all_to_all(restore(event_grad), "exp", split_axis=0, concat_axis=0, tiled=True),
    )
    out_rows = (
        back_out.reshape(experts * capacity, columns)[targets]
        .reshape(rows_here, fanout, columns)
        .astype(jnp.float32)
    )
    grad_rows = (
        back_grad.reshape(experts * capacity, columns)[targets]
        .reshape(rows_here, fanout, columns)
        .astype(jnp.float32)
    )
    mixed = jnp.sum(event_weights[:, :, None] * out_rows, axis=1).astype(jnp.bfloat16)
    token_grad = jnp.sum(grad_rows, axis=1).astype(jnp.bfloat16)
    weight_part = jnp.einsum("td,tkd->tk", cotangent.astype(jnp.float32), out_rows)
    weight_grad = lax.psum(weight_part, "ctx")
    return (mixed, token_grad, weight_grad)


def fused(
    sizes,
    routes_ref, weights_ref, tokens_ref, cot_ref, gate_hbm, up_hbm, down_hbm,
    mixed_ref, grad_ref, wgrad_ref,
    gate_w, up_w, down_w, x_send, x_recv, rt_recv, cots, part, shares, acts, grads, saved,
    stack, landing, all_picks, pair_picks, slot_w, wg_send, wg_recv, wg_parts,
    load_sem, x_ssem, x_rsem, rt_ssem, rt_rsem, far_up, far_down, far_rsem, sib_ssem, sib_rsem,
    rs_ssem, rs_rsem, bk_ssem, bk_rsem, ag_ssem, ag_rsem, gg_ssem, gg_rsem,
    res_ssem, res_rsem, wgz_ssem, wgz_rsem, wg_ssem, wg_rsem,
):
    owners, splits, capacity, rows, columns, hidden = sizes
    part_f = hidden // splits
    half = rows // 2
    z, c, r = lax.axis_index("exp"), lax.axis_index("ctx"), lax.axis_index("rep")
    bf, f32 = jnp.bfloat16, jnp.float32

    def expert_at(d):
        return lax.rem(z + d, owners)

    def source_at(d):
        return lax.rem(z - d + owners, owners)

    def peer_at(q):
        return lax.rem(c + q, splits)

    def from_peer(q):
        return lax.rem(c - q + splits, splits)

    def remote(src, dst, ssem, rsem, **where):
        return pltpu.make_async_remote_copy(
            src_ref=src, dst_ref=dst, send_sem=ssem, recv_sem=rsem,
            device_id=where, device_id_type=pl.DeviceIdType.MESH,
        )

    loads = [
        pltpu.make_async_copy(gate_hbm.at[0], gate_w, load_sem.at[0]),
        pltpu.make_async_copy(up_hbm.at[0], up_w, load_sem.at[1]),
        pltpu.make_async_copy(down_hbm.at[0], down_w, load_sem.at[2]),
    ]
    for load in loads:
        load.start()

    barrier = pltpu.get_barrier_semaphore()
    for d in range(1, owners):
        pl.semaphore_signal(barrier, inc=1, device_id={"exp": expert_at(d)}, device_id_type=pl.DeviceIdType.MESH)
    for q in range(1, splits):
        pl.semaphore_signal(barrier, inc=1, device_id={"ctx": peer_at(q)}, device_id_type=pl.DeviceIdType.MESH)
    pl.semaphore_signal(barrier, inc=1, device_id={"rep": 1 - r}, device_id_type=pl.DeviceIdType.MESH)

    routes = routes_ref[...]
    event_w = weights_ref[...]
    row_i = lax.broadcasted_iota(jnp.int32, (rows, rows), 0)
    col_i = lax.broadcasted_iota(jnp.int32, (rows, rows), 1)
    upper = (row_i < col_i).astype(f32).astype(bf)
    experts_i = lax.broadcasted_iota(jnp.int32, (16, rows), 0)
    rt_recv[0, 0:2] = routes.astype(f32)
    rt_recv[0, 2:4] = event_w
    rt_recv[0, 4:] = jnp.zeros((4, rows), f32)

    end = z // 2
    partner = z + 1 - 2 * lax.rem(z, 2)
    inner = (z == 1) | (z == 2)

    def line(i):
        other = (z, partner, 2 - end, 3 * (1 - end))[i]
        return other, lax.rem(z - other + owners, owners), lax.rem(other - z + owners, owners)

    def picks(d, expert):
        r0, r1 = rt_recv[d, 0:1], rt_recv[d, 1:2]
        experts_f = experts_i.astype(f32)
        named = ((experts_f == r0) | (experts_f == r1)).astype(f32)
        pos = jnp.dot(named.astype(bf), upper, preferred_element_type=f32)
        mine = experts_i == expert
        pos_e = jnp.sum(jnp.where(mine, pos, 0.0), axis=0, keepdims=True)
        has_e = jnp.sum(jnp.where(mine, named, 0.0), axis=0, keepdims=True)
        place = lax.broadcasted_iota(jnp.int32, (capacity, rows), 0).astype(f32)
        return (place == pos_e) & (has_e > 0.5)

    def as_bf(mask):
        return mask.astype(f32).astype(bf)

    pl.semaphore_wait(barrier, owners + splits - 1)

    steps = range(1, owners)

    def rt(i):
        other, _, d = line(i)
        return remote(rt_recv.at[0], rt_recv.at[d], rt_ssem.at[i], rt_rsem.at[d], exp=other)

    def send_x(i):
        other, _, d = line(i)
        return remote(x_send.at[i], x_recv.at[d], x_ssem.at[i], x_rsem.at[d], exp=other)

    def got_x(i):
        other, d, _ = line(i)
        remote(rt_recv.at[0], rt_recv.at[d], rt_ssem.at[i], rt_rsem.at[d], exp=other).wait_recv()
        remote(x_send.at[i], x_recv.at[d], x_ssem.at[i], x_rsem.at[d], exp=other).wait_recv()
        return d

    for i in steps:
        rt(i).start()
    for i in steps:
        x_send[i] = jnp.dot(as_bf(picks(0, line(i)[0])), tokens_ref[...], preferred_element_type=f32).astype(bf)
        send_x(i).start()

    my_half = pl.ds(pl.multiple_of(r * half, half), half)

    def far(src, j, going_up):
        sem = far_up if going_up else far_down
        return remote(src, cots.at[j, my_half], sem.at[j], far_rsem.at[j], exp=z + (1 if going_up else -1))

    def sibling(j):
        return remote(cots.at[j, my_half], cots.at[j, my_half], sib_ssem.at[j], sib_rsem.at[j], rep=1 - r)

    @pl.when(z < owners - 1)
    def _():
        far(cot_ref.at[my_half], z, True).start()

    @pl.when(z > 0)
    def _():
        far(cot_ref.at[my_half], z, False).start()

    cots[z] = cot_ref[...]
    x_recv[0] = jnp.dot(as_bf(picks(0, z)), tokens_ref[...], preferred_element_type=f32).astype(bf)

    def pass_on(d):
        @pl.when(z - d >= 0)
        def _():
            j = z - d
            far(cots.at[j, my_half], j, True).wait_recv()

            @pl.when(z < owners - 1)
            def _():
                far(cots.at[j, my_half], j, True).start()

            sibling(j).start()

        @pl.when(z + d < owners)
        def _():
            j = z + d
            far(cots.at[j, my_half], j, False).wait_recv()

            @pl.when(z > 0)
            def _():
                far(cots.at[j, my_half], j, False).start()

            sibling(j).start()

    for load in loads:
        load.wait()

    def slices(p):
        return slice(p * part_f, (p + 1) * part_f)

    def first(d):
        x = x_recv[d]
        for p in range(splits):
            part[d, p, 0:capacity] = jnp.dot(x, gate_w[:, slices(p)], preferred_element_type=f32).astype(bf)
            part[d, p, capacity:2 * capacity] = jnp.dot(x, up_w[:, slices(p)], preferred_element_type=f32).astype(bf)

    def back(i, d):
        pick = pair_picks[i]
        rows_in = jnp.dot(pick, cots[source_at(d)], preferred_element_type=f32).astype(bf)
        for p in range(splits):
            part[d, p, 2 * capacity:3 * capacity] = lax.dot_general(
                rows_in, down_w[slices(p), :], (((1,), (1,)), ((), ())), preferred_element_type=f32
            ).astype(bf)

    def rs(d, q):
        at = pl.ds(0, 2 * capacity)
        return remote(part.at[d, peer_at(q), at], shares.at[d, q, at], rs_ssem.at[d, q], rs_rsem.at[d, q], ctx=peer_at(q))

    def bk(d, q):
        at = pl.ds(2 * capacity, capacity)
        return remote(part.at[d, peer_at(q), at], shares.at[d, q, at], bk_ssem.at[d, q], bk_rsem.at[d, q], ctx=peer_at(q))

    def ag(d, q):
        return remote(acts.at[d, c], acts.at[d, c], ag_ssem.at[d, q], ag_rsem.at[d, q], ctx=peer_at(q))

    def gg(d, q):
        return remote(grads.at[d, c], grads.at[d, c], gg_ssem.at[d, q], gg_rsem.at[d, q], ctx=peer_at(q))

    def result(k, i):
        other, d, _ = line(i)
        at = pl.ds(pl.multiple_of(d * capacity, capacity), capacity)
        return remote(stack.at[k, i], landing.at[k, at], res_ssem.at[k, i], res_rsem.at[k, d], exp=other)

    def got_result(k, i):
        other, _, d = line(i)
        at = pl.ds(pl.multiple_of(d * capacity, capacity), capacity)
        return remote(stack.at[k, i], landing.at[k, at], res_ssem.at[k, i], res_rsem.at[k, d], exp=other)

    def hand_on(k, i):
        if i:
            result(k, i).start()

    step = 256 if columns % 256 == 0 else columns

    def wgz(i):
        other, d, _ = line(i)
        return remote(wg_send.at[i], wg_recv.at[d], wgz_ssem.at[i], wgz_rsem.at[d], exp=other)

    others = range(1, splits)

    def activate_block(d):
        for q in others:
            rs(d, q).wait_recv()
        both = part[d, c, 0:2 * capacity].astype(f32)
        for q in others:
            both = both + shares[d, q, 0:2 * capacity].astype(f32)
        saved[d] = both
        gate_pre, up_pre = both[0:capacity], both[capacity:]
        acts[d, c] = (gate_pre * jax.nn.sigmoid(gate_pre) * up_pre).astype(bf)
        for q in others:
            ag(d, q).start()

    def back_block(i):
        d = 0
        if i > 0:
            other, d, _ = line(i)
            sibling(other).wait_recv()
        back(i, d)
        for q in others:
            bk(d, q).start()

    def first_block(i):
        d = got_x(i) if i else 0
        first(d)
        mine = picks(d, z)
        pair_picks[i] = as_bf(mine)
        expert = z.astype(f32)
        named = jnp.where(rt_recv[d, 0:2] == expert, rt_recv[d, 2:4], 0.0)
        slot_w[i] = jnp.sum(jnp.where(mine, jnp.sum(named, axis=0, keepdims=True), 0.0), axis=1, keepdims=True)
        for q in others:
            rs(d, q).start()

    def slot(i):
        return line(i)[1] if i else 0

    def out_block(i):
        d = slot(i)
        for q in others:
            ag(d, q).wait_recv()
        act = jnp.concatenate([acts[d, p] for p in range(splits)], axis=1)
        weight = slot_w[i]
        for n in range(0, columns, step):
            into = stack.at[0, i] if i else landing.at[0, 0:capacity]
            into[:, n:n + step] = (
                weight * jnp.dot(act, down_w[:, n:n + step], preferred_element_type=f32)
            ).astype(bf)
        hand_on(0, i)

    def grad_block(i):
        d = slot(i)
        for q in others:
            bk(d, q).wait_recv()
        back_pre = part[d, c, 2 * capacity:].astype(f32)
        for q in others:
            back_pre = back_pre + shares[d, q, 2 * capacity:].astype(f32)
        gate_pre, up_pre = saved[d, 0:capacity], saved[d, capacity:]
        squash = jax.nn.sigmoid(gate_pre)
        per_slot = jnp.sum(acts[d, c].astype(f32) * back_pre, axis=1, keepdims=True)
        per_token = jnp.sum(jnp.where(pair_picks[i].astype(f32) > 0.5, per_slot, 0.0), axis=0, keepdims=True)
        where_to = wg_send if i else wg_recv
        where_to[i] = jnp.broadcast_to(per_token, (8, rows))
        if i:
            wgz(i).start()
        back_pre = slot_w[i] * back_pre
        grads[d, c, 0:capacity] = (back_pre * up_pre * squash * (1.0 + gate_pre * (1.0 - squash))).astype(bf)
        grads[d, c, capacity:] = (back_pre * gate_pre * squash).astype(bf)
        for q in others:
            gg(d, q).start()

    def eg_block(i):
        d = slot(i)
        for q in others:
            gg(d, q).wait_recv()
        gate_g = jnp.concatenate([grads[d, p, 0:capacity] for p in range(splits)], axis=1)
        up_g = jnp.concatenate([grads[d, p, capacity:] for p in range(splits)], axis=1)
        for n in range(0, columns, step):
            nt = (((1,), (1,)), ((), ()))
            into = stack.at[1, i] if i else landing.at[1, 0:capacity]
            into[:, n:n + step] = (
                lax.dot_general(gate_g, gate_w[n:n + step], nt, preferred_element_type=f32)
                + lax.dot_general(up_g, up_w[n:n + step], nt, preferred_element_type=f32)
            ).astype(bf)
        hand_on(1, i)

    first_block(0)
    back_block(0)
    for d in range(owners):
        all_picks[:, d * capacity:(d + 1) * capacity] = as_bf(picks(0, expert_at(d))).astype(f32).T.astype(bf)
    first_block(1)
    activate_block(slot(0))
    pass_on(1)
    first_block(2)
    activate_block(slot(1))
    out_block(1)
    first_block(3)
    activate_block(slot(2))
    pass_on(2)
    out_block(2)
    back_block(1)
    activate_block(slot(3))
    out_block(3)
    grad_block(0)
    grad_block(1)
    pass_on(3)
    back_block(2)
    back_block(3)
    eg_block(1)
    grad_block(2)
    grad_block(3)
    eg_block(2)
    eg_block(3)
    out_block(0)
    eg_block(0)

    def wg(q):
        return remote(wg_parts.at[0], wg_parts.at[q], wg_ssem.at[q], wg_rsem.at[q], ctx=peer_at(q))

    acc = jnp.zeros(routes.shape, f32)
    for i in range(owners):
        expert, _, d = line(i)
        if i:
            remote(wg_send.at[i], wg_recv.at[d], wgz_ssem.at[i], wgz_rsem.at[d], exp=expert).wait_recv()
        acc = acc + jnp.where(routes == expert, wg_recv[d if i else 0, 0:1], 0.0)
    wg_parts[0, 0:routes.shape[0]] = acc
    wg_parts[0, routes.shape[0]:] = jnp.zeros((8 - routes.shape[0], rows), f32)
    for q in others:
        wg(q).start()

    def collect(k, into):
        for i in steps:
            got_result(k, i).wait_recv()
        for n in range(0, columns, step):
            at = slice(n, n + step)
            into[:, at] = jnp.dot(all_picks[...], landing[k, :, at], preferred_element_type=f32).astype(bf)

    collect(0, mixed_ref)
    for q in others:
        wg(q).wait_recv()
        acc = acc + wg_parts[q, 0:routes.shape[0]]
    wgrad_ref[...] = acc
    collect(1, grad_ref)

    for i in steps:
        send_x(i).wait_send()
        rt(i).wait_send()
        wgz(i).wait_send()
        for k in range(2):
            result(k, i).wait_send()
    for q in others:
        wg(q).wait_send()
        for d in range(owners):
            rs(d, q).wait_send()
            bk(d, q).wait_send()
            ag(d, q).wait_send()
            gg(d, q).wait_send()

    @pl.when(z < owners - 1)
    def _():
        far(cot_ref.at[my_half], z, True).wait_send()

    @pl.when(z > 0)
    def _():
        far(cot_ref.at[my_half], z, False).wait_send()

    for d in range(1, owners):
        @pl.when(z - d >= 0)
        def _():
            @pl.when(z < owners - 1)
            def _():
                far(cots.at[z - d, my_half], z - d, True).wait_send()

            sibling(z - d).wait_send()

        @pl.when(z + d < owners)
        def _():
            @pl.when(z > 0)
            def _():
                far(cots.at[z + d, my_half], z + d, False).wait_send()

            sibling(z + d).wait_send()


def hand_over(*refs):
    for source, target in zip(refs[:3], refs[3:]):
        target[...] = source[...]


def shards_fused(tokens, routes, event_weights, cotangent, w_gate, w_up, w_down):
    owners, splits = lax.axis_size("exp"), lax.axis_size("ctx")
    _, columns, hidden = w_gate.shape
    rows, fanout = routes.shape
    capacity = max(2, 5 * rows * fanout // (4 * owners))
    part_f = hidden // splits
    sizes = (owners, splits, capacity, rows, columns, hidden)
    bf, f32 = jnp.bfloat16, jnp.float32
    vmem, dma = pltpu.VMEM, pltpu.SemaphoreType.DMA
    full = pl.BlockSpec(memory_space=pltpu.VMEM)
    anywhere = pl.BlockSpec(memory_space=pl.ANY)
    per_block = dma((owners,))
    per_pair = dma((owners, splits))
    moved = owners * capacity * columns
    results = pl.pallas_call(
        functools.partial(fused, sizes),
        out_shape=(
            jax.ShapeDtypeStruct((rows, columns), bf),
            jax.ShapeDtypeStruct((rows, columns), bf),
            jax.ShapeDtypeStruct((fanout, rows), f32),
        ),
        in_specs=[full, full, full, full, anywhere, anywhere, anywhere],
        out_specs=(full, full, full),
        scratch_shapes=[
            vmem((columns, hidden), bf), vmem((columns, hidden), bf), vmem((hidden, columns), bf),
            vmem((owners, capacity, columns), bf), vmem((owners, capacity, columns), bf),
            vmem((owners, 8, rows), f32),
            vmem((owners, rows, columns), bf),
            vmem((owners, splits, 3 * capacity, part_f), bf),
            vmem((owners, splits, 3 * capacity, part_f), bf),
            vmem((owners, splits, capacity, part_f), bf),
            vmem((owners, splits, 2 * capacity, part_f), bf),
            vmem((owners, 2 * capacity, part_f), f32),
            vmem((2, owners, capacity, columns), bf), vmem((2, owners * capacity, columns), bf),
            vmem((rows, owners * capacity), bf),
            vmem((owners, capacity, rows), bf), vmem((owners, capacity, 1), f32),
            vmem((owners, 8, rows), f32), vmem((owners, 8, rows), f32), vmem((splits, 8, rows), f32),
            dma((3,)), per_block, per_block, per_block, per_block,
            per_block, per_block, per_block, per_block, per_block,
            per_pair, per_pair, per_pair, per_pair, per_pair, per_pair, per_pair, per_pair,
            dma((2, owners)), dma((2, owners)), per_block, per_block, dma((splits,)), dma((splits,)),
        ],
        compiler_params=pltpu.CompilerParams(
            collective_id=0, has_side_effects=True, vmem_limit_bytes=56 * 1024 * 1024
        ),
        cost_estimate=pl.CostEstimate(
            flops=12 * moved * hidden, bytes_accessed=6 * columns * hidden, transcendentals=0
        ),
    )(routes.T, event_weights.T, tokens, cotangent, w_gate, w_up, w_down)
    mixed, token_grad, weight_grad = pl.pallas_call(
        hand_over,
        out_shape=tuple(jax.ShapeDtypeStruct(x.shape, x.dtype) for x in results),
        in_specs=[full] * 3,
        out_specs=(full,) * 3,
        cost_estimate=pl.CostEstimate(flops=0, bytes_accessed=8 * rows * columns, transcendentals=0),
    )(*results)
    return mixed, token_grad, weight_grad.T


def fits(mesh, w_gate, routes):
    owners, splits, cores = mesh.shape["exp"], mesh.shape["ctx"], mesh.shape["rep"]
    experts, depth, hidden = w_gate.shape
    rows, fanout = routes.shape[0] // (owners * cores), routes.shape[1]
    capacity = max(2, 5 * rows * fanout // (4 * experts))
    columns = depth // splits
    return (
        experts == owners and owners == 4 and splits > 1 and cores == 2 and fanout == 2
        and rows == 128 and capacity % 16 == 0 and columns % 128 == 0 and hidden % (128 * splits) == 0
        and 6 * columns * hidden <= 16 * 1024 * 1024
    )


def solution(mesh):
    in_specs = (
        P(("rep", "exp"), "ctx"),
        P(("rep", "exp"), None),
        P(("rep", "exp"), None),
        P("exp", "ctx"),
        P("exp", "ctx", None),
        P("exp", "ctx", None),
        P("exp", None, "ctx"),
    )
    out_specs = (P(("rep", "exp"), "ctx"), P(("rep", "exp"), "ctx"), P(("rep", "exp"), None))

    def run(tokens, routes, event_weights, cotangent, w_gate, w_up, w_down):
        body = shards_fused if fits(mesh, w_gate, routes) else shards
        mapped = jax.shard_map(body, mesh=mesh, in_specs=in_specs, out_specs=out_specs, check_vma=False)
        return mapped(tokens, routes, event_weights, cotangent, w_gate, w_up, w_down)

    return run
```

```python
import functools

import jax
import jax.numpy as jnp
from jax import lax
from jax.experimental import pallas as pl
from jax.experimental.pallas import tpu as pltpu
from jax.sharding import PartitionSpec as P


def activate(gate_pre, up_pre, back_pre):
    squash = jax.nn.sigmoid(gate_pre)
    hidden_act = (gate_pre * squash * up_pre).astype(jnp.bfloat16)
    grad_gate = (back_pre * up_pre * squash * (1.0 + gate_pre * (1.0 - squash))).astype(
        jnp.bfloat16
    )
    grad_up = (back_pre * gate_pre * squash).astype(jnp.bfloat16)
    return (hidden_act, grad_gate, grad_up)


def shards(tokens, routes, event_weights, cotangent, w_gate, w_up, w_down):
    owners = lax.axis_size("exp")
    owned, columns, hidden = w_gate.shape
    experts = owned * owners
    rows_here, fanout = routes.shape
    capacity = max(2, 5 * rows_here * fanout // (4 * experts))
    slot_count = owners * capacity
    routes_flat = routes.reshape(-1)
    onehot = (routes_flat[:, None] == jnp.arange(experts, dtype=jnp.int32)[None, :]).astype(
        jnp.int32
    )
    places = jnp.sum((jnp.cumsum(onehot, axis=0) - onehot) * onehot, axis=1)
    targets = routes_flat * capacity + places
    token_rows = jnp.repeat(tokens, fanout, axis=0)
    cot_rows = (
        event_weights.reshape(-1, 1) * jnp.repeat(cotangent.astype(jnp.float32), fanout, axis=0)
    ).astype(jnp.bfloat16)
    send_tokens = jnp.zeros((experts * capacity, columns), jnp.bfloat16).at[targets].set(token_rows)
    send_cots = jnp.zeros((experts * capacity, columns), jnp.bfloat16).at[targets].set(cot_rows)
    send_tokens = send_tokens.reshape(owners, owned * capacity, columns)
    send_cots = send_cots.reshape(owners, owned * capacity, columns)
    recv_tokens, recv_cots = (
        lax.all_to_all(send_tokens, "exp", split_axis=0, concat_axis=0, tiled=True),
        lax.all_to_all(send_cots, "exp", split_axis=0, concat_axis=0, tiled=True),
    )

    def arrange(buffer):
        return (
            buffer.reshape(owners, owned, capacity, columns)
            .transpose(1, 0, 2, 3)
            .reshape(owned, slot_count, columns)
        )

    expert_in = arrange(recv_tokens)
    expert_cot = arrange(recv_cots)
    shares = lax.psum_scatter(
        jnp.stack(
            [
                jnp.einsum("jsd,jdf->fjs", expert_in, w_gate, preferred_element_type=jnp.float32),
                jnp.einsum("jsd,jdf->fjs", expert_in, w_up, preferred_element_type=jnp.float32),
                jnp.einsum("jsd,jfd->fjs", expert_cot, w_down, preferred_element_type=jnp.float32),
            ],
            axis=1,
        ).astype(jnp.bfloat16),
        "ctx",
        scatter_dimension=0,
        tiled=True,
    ).astype(jnp.float32)
    hidden_share, gate_share, up_share = activate(shares[:, 0], shares[:, 1], shares[:, 2])
    hidden_act, grad_gate, grad_up = (
        lax.all_gather(hidden_share, "ctx", axis=0, tiled=True),
        lax.all_gather(gate_share, "ctx", axis=0, tiled=True),
        lax.all_gather(up_share, "ctx", axis=0, tiled=True),
    )
    expert_out = jnp.einsum(
        "fjs,jfd->jsd", hidden_act, w_down, preferred_element_type=jnp.float32
    ).astype(jnp.bfloat16)
    event_grad = (
        jnp.einsum("fjs,jdf->jsd", grad_gate, w_gate, preferred_element_type=jnp.float32)
        + jnp.einsum("fjs,jdf->jsd", grad_up, w_up, preferred_element_type=jnp.float32)
    ).astype(jnp.bfloat16)

    def restore(buffer):
        return (
            buffer.reshape(owned, owners, capacity, columns)
            .transpose(1, 0, 2, 3)
            .reshape(owners, owned * capacity, columns)
        )

    back_out, back_grad = (
        lax.all_to_all(restore(expert_out), "exp", split_axis=0, concat_axis=0, tiled=True),
        lax.all_to_all(restore(event_grad), "exp", split_axis=0, concat_axis=0, tiled=True),
    )
    out_rows = (
        back_out.reshape(experts * capacity, columns)[targets]
        .reshape(rows_here, fanout, columns)
        .astype(jnp.float32)
    )
    grad_rows = (
        back_grad.reshape(experts * capacity, columns)[targets]
        .reshape(rows_here, fanout, columns)
        .astype(jnp.float32)
    )
    mixed = jnp.sum(event_weights[:, :, None] * out_rows, axis=1).astype(jnp.bfloat16)
    token_grad = jnp.sum(grad_rows, axis=1).astype(jnp.bfloat16)
    weight_part = jnp.einsum("td,tkd->tk", cotangent.astype(jnp.float32), out_rows)
    weight_grad = lax.psum(weight_part, "ctx")
    return (mixed, token_grad, weight_grad)


def fused(
    sizes,
    routes_ref, weights_ref, tokens_ref, cot_ref, gate_hbm, up_hbm, down_hbm,
    mixed_ref, grad_ref, wgrad_ref,
    gate_w, up_w, down_w, x_send, x_recv, rt_recv, cots, part, shares, acts, grads, saved,
    stack, landing, all_picks, pair_picks, slot_w, wg_send, wg_recv, wg_parts,
    load_sem, x_ssem, x_rsem, rt_ssem, rt_rsem, far_up, far_down, far_rsem, sib_ssem, sib_rsem,
    rs_ssem, rs_rsem, bk_ssem, bk_rsem, ag_ssem, ag_rsem, gg_ssem, gg_rsem,
    res_ssem, res_rsem, wgz_ssem, wgz_rsem, wg_ssem, wg_rsem,
):
    owners, splits, capacity, rows, columns, hidden = sizes
    part_f = hidden // splits
    half = rows // 2
    z, c, r = lax.axis_index("exp"), lax.axis_index("ctx"), lax.axis_index("rep")
    bf, f32 = jnp.bfloat16, jnp.float32

    def expert_at(d):
        return lax.rem(z + d, owners)

    def source_at(d):
        return lax.rem(z - d + owners, owners)

    def peer_at(q):
        return lax.rem(c + q, splits)

    def from_peer(q):
        return lax.rem(c - q + splits, splits)

    def remote(src, dst, ssem, rsem, **where):
        return pltpu.make_async_remote_copy(
            src_ref=src, dst_ref=dst, send_sem=ssem, recv_sem=rsem,
            device_id=where, device_id_type=pl.DeviceIdType.MESH,
        )

    loads = [
        pltpu.make_async_copy(gate_hbm.at[0], gate_w, load_sem.at[0]),
        pltpu.make_async_copy(up_hbm.at[0], up_w, load_sem.at[1]),
        pltpu.make_async_copy(down_hbm.at[0], down_w, load_sem.at[2]),
    ]
    for load in loads:
        load.start()

    barrier = pltpu.get_barrier_semaphore()
    for d in range(1, owners):
        pl.semaphore_signal(barrier, inc=1, device_id={"exp": expert_at(d)}, device_id_type=pl.DeviceIdType.MESH)
    for q in range(1, splits):
        pl.semaphore_signal(barrier, inc=1, device_id={"ctx": peer_at(q)}, device_id_type=pl.DeviceIdType.MESH)
    pl.semaphore_signal(barrier, inc=1, device_id={"rep": 1 - r}, device_id_type=pl.DeviceIdType.MESH)

    routes = routes_ref[...]
    event_w = weights_ref[...]
    row_i = lax.broadcasted_iota(jnp.int32, (rows, rows), 0)
    col_i = lax.broadcasted_iota(jnp.int32, (rows, rows), 1)
    upper = (row_i < col_i).astype(f32).astype(bf)
    experts_i = lax.broadcasted_iota(jnp.int32, (16, rows), 0)
    rt_recv[0, 0:2] = routes.astype(f32)
    rt_recv[0, 2:4] = event_w
    rt_recv[0, 4:] = jnp.zeros((4, rows), f32)

    end = z // 2
    partner = z + 1 - 2 * lax.rem(z, 2)
    inner = (z == 1) | (z == 2)

    def line(i):
        other = (z, partner, 2 - end, 3 * (1 - end))[i]
        return other, lax.rem(z - other + owners, owners), lax.rem(other - z + owners, owners)

    def picks(d, expert):
        r0, r1 = rt_recv[d, 0:1], rt_recv[d, 1:2]
        experts_f = experts_i.astype(f32)
        named = ((experts_f == r0) | (experts_f == r1)).astype(f32)
        pos = jnp.dot(named.astype(bf), upper, preferred_element_type=f32)
        mine = experts_i == expert
        pos_e = jnp.sum(jnp.where(mine, pos, 0.0), axis=0, keepdims=True)
        has_e = jnp.sum(jnp.where(mine, named, 0.0), axis=0, keepdims=True)
        place = lax.broadcasted_iota(jnp.int32, (capacity, rows), 0).astype(f32)
        return (place == pos_e) & (has_e > 0.5)

    def as_bf(mask):
        return mask.astype(f32).astype(bf)

    pl.semaphore_wait(barrier, owners + splits - 1)

    steps = range(1, owners)

    def rt(i):
        other, _, d = line(i)
        return remote(rt_recv.at[0], rt_recv.at[d], rt_ssem.at[i], rt_rsem.at[d], exp=other)

    def send_x(i):
        other, _, d = line(i)
        return remote(x_send.at[i], x_recv.at[d], x_ssem.at[i], x_rsem.at[d], exp=other)

    def got_x(i):
        other, d, _ = line(i)
        remote(rt_recv.at[0], rt_recv.at[d], rt_ssem.at[i], rt_rsem.at[d], exp=other).wait_recv()
        remote(x_send.at[i], x_recv.at[d], x_ssem.at[i], x_rsem.at[d], exp=other).wait_recv()
        return d

    for i in steps:
        rt(i).start()
    for i in steps:
        x_send[i] = jnp.dot(as_bf(picks(0, line(i)[0])), tokens_ref[...], preferred_element_type=f32).astype(bf)
        send_x(i).start()

    my_half = pl.ds(pl.multiple_of(r * half, half), half)

    def far(src, j, going_up):
        sem = far_up if going_up else far_down
        return remote(src, cots.at[j, my_half], sem.at[j], far_rsem.at[j], exp=z + (1 if going_up else -1))

    def sibling(j):
        return remote(cots.at[j, my_half], cots.at[j, my_half], sib_ssem.at[j], sib_rsem.at[j], rep=1 - r)

    @pl.when(z < owners - 1)
    def _():
        far(cot_ref.at[my_half], z, True).start()

    @pl.when(z > 0)
    def _():
        far(cot_ref.at[my_half], z, False).start()

    cots[z] = cot_ref[...]
    x_recv[0] = jnp.dot(as_bf(picks(0, z)), tokens_ref[...], preferred_element_type=f32).astype(bf)

    def pass_on(d):
        @pl.when(z - d >= 0)
        def _():
            j = z - d
            far(cots.at[j, my_half], j, True).wait_recv()

            @pl.when(z < owners - 1)
            def _():
                far(cots.at[j, my_half], j, True).start()

            sibling(j).start()

        @pl.when(z + d < owners)
        def _():
            j = z + d
            far(cots.at[j, my_half], j, False).wait_recv()

            @pl.when(z > 0)
            def _():
                far(cots.at[j, my_half], j, False).start()

            sibling(j).start()

    for load in loads:
        load.wait()

    def slices(p):
        return slice(p * part_f, (p + 1) * part_f)

    def first(d):
        x = x_recv[d]
        for p in range(splits):
            part[d, p, 0:capacity] = jnp.dot(x, gate_w[:, slices(p)], preferred_element_type=f32).astype(bf)
            part[d, p, capacity:2 * capacity] = jnp.dot(x, up_w[:, slices(p)], preferred_element_type=f32).astype(bf)

    def back(i, d):
        pick = pair_picks[i]
        rows_in = jnp.dot(pick, cots[source_at(d)], preferred_element_type=f32).astype(bf)
        for p in range(splits):
            part[d, p, 2 * capacity:3 * capacity] = lax.dot_general(
                rows_in, down_w[slices(p), :], (((1,), (1,)), ((), ())), preferred_element_type=f32
            ).astype(bf)

    def rs(d, q):
        at = pl.ds(0, 2 * capacity)
        return remote(part.at[d, peer_at(q), at], shares.at[d, q, at], rs_ssem.at[d, q], rs_rsem.at[d, q], ctx=peer_at(q))

    def bk(d, q):
        at = pl.ds(2 * capacity, capacity)
        return remote(part.at[d, peer_at(q), at], shares.at[d, q, at], bk_ssem.at[d, q], bk_rsem.at[d, q], ctx=peer_at(q))

    def ag(d, q):
        return remote(acts.at[d, c], acts.at[d, c], ag_ssem.at[d, q], ag_rsem.at[d, q], ctx=peer_at(q))

    def gg(d, q):
        return remote(grads.at[d, c], grads.at[d, c], gg_ssem.at[d, q], gg_rsem.at[d, q], ctx=peer_at(q))

    def result(k, i):
        other, d, _ = line(i)
        at = pl.ds(pl.multiple_of(d * capacity, capacity), capacity)
        return remote(stack.at[k, i], landing.at[k, at], res_ssem.at[k, i], res_rsem.at[k, d], exp=other)

    def got_result(k, i):
        other, _, d = line(i)
        at = pl.ds(pl.multiple_of(d * capacity, capacity), capacity)
        return remote(stack.at[k, i], landing.at[k, at], res_ssem.at[k, i], res_rsem.at[k, d], exp=other)

    def hand_on(k, i):
        if i:
            result(k, i).start()

    step = 256 if columns % 256 == 0 else columns

    def wgz(i):
        other, d, _ = line(i)
        return remote(wg_send.at[i], wg_recv.at[d], wgz_ssem.at[i], wgz_rsem.at[d], exp=other)

    others = range(1, splits)

    def activate_block(d):
        for q in others:
            rs(d, q).wait_recv()
        both = part[d, c, 0:2 * capacity].astype(f32)
        for q in others:
            both = both + shares[d, q, 0:2 * capacity].astype(f32)
        saved[d] = both
        gate_pre, up_pre = both[0:capacity], both[capacity:]
        acts[d, c] = (gate_pre * jax.nn.sigmoid(gate_pre) * up_pre).astype(bf)
        for q in others:
            ag(d, q).start()

    def back_block(i):
        d = 0
        if i > 0:
            other, d, _ = line(i)
            sibling(other).wait_recv()
        back(i, d)
        for q in others:
            bk(d, q).start()

    def first_block(i):
        d = got_x(i) if i else 0
        first(d)
        mine = picks(d, z)
        pair_picks[i] = as_bf(mine)
        expert = z.astype(f32)
        named = jnp.where(rt_recv[d, 0:2] == expert, rt_recv[d, 2:4], 0.0)
        slot_w[i] = jnp.sum(jnp.where(mine, jnp.sum(named, axis=0, keepdims=True), 0.0), axis=1, keepdims=True)
        for q in others:
            rs(d, q).start()

    def slot(i):
        return line(i)[1] if i else 0

    def out_block(i):
        d = slot(i)
        for q in others:
            ag(d, q).wait_recv()
        act = jnp.concatenate([acts[d, p] for p in range(splits)], axis=1)
        weight = slot_w[i]
        for n in range(0, columns, step):
            into = stack.at[0, i] if i else landing.at[0, 0:capacity]
            into[:, n:n + step] = (
                weight * jnp.dot(act, down_w[:, n:n + step], preferred_element_type=f32)
            ).astype(bf)
        hand_on(0, i)

    def grad_block(i):
        d = slot(i)
        for q in others:
            bk(d, q).wait_recv()
        back_pre = part[d, c, 2 * capacity:].astype(f32)
        for q in others:
            back_pre = back_pre + shares[d, q, 2 * capacity:].astype(f32)
        gate_pre, up_pre = saved[d, 0:capacity], saved[d, capacity:]
        squash = jax.nn.sigmoid(gate_pre)
        per_slot = jnp.sum(acts[d, c].astype(f32) * back_pre, axis=1, keepdims=True)
        per_token = jnp.sum(jnp.where(pair_picks[i].astype(f32) > 0.5, per_slot, 0.0), axis=0, keepdims=True)
        where_to = wg_send if i else wg_recv
        where_to[i] = jnp.broadcast_to(per_token, (8, rows))
        if i:
            wgz(i).start()
        back_pre = slot_w[i] * back_pre
        grads[d, c, 0:capacity] = (back_pre * up_pre * squash * (1.0 + gate_pre * (1.0 - squash))).astype(bf)
        grads[d, c, capacity:] = (back_pre * gate_pre * squash).astype(bf)
        for q in others:
            gg(d, q).start()

    def eg_block(i):
        d = slot(i)
        for q in others:
            gg(d, q).wait_recv()
        gate_g = jnp.concatenate([grads[d, p, 0:capacity] for p in range(splits)], axis=1)
        up_g = jnp.concatenate([grads[d, p, capacity:] for p in range(splits)], axis=1)
        for n in range(0, columns, step):
            nt = (((1,), (1,)), ((), ()))
            into = stack.at[1, i] if i else landing.at[1, 0:capacity]
            into[:, n:n + step] = (
                lax.dot_general(gate_g, gate_w[n:n + step], nt, preferred_element_type=f32)
                + lax.dot_general(up_g, up_w[n:n + step], nt, preferred_element_type=f32)
            ).astype(bf)
        hand_on(1, i)

    first_block(0)
    back_block(0)
    for d in range(owners):
        all_picks[:, d * capacity:(d + 1) * capacity] = as_bf(picks(0, expert_at(d))).astype(f32).T.astype(bf)
    first_block(1)
    activate_block(slot(0))
    pass_on(1)
    first_block(2)
    activate_block(slot(1))
    out_block(1)
    first_block(3)
    activate_block(slot(2))
    pass_on(2)
    out_block(2)
    back_block(1)
    activate_block(slot(3))
    out_block(3)
    grad_block(0)
    grad_block(1)
    pass_on(3)
    back_block(2)
    back_block(3)
    out_block(0)
    grad_block(2)
    grad_block(3)
    eg_block(1)
    eg_block(2)
    eg_block(3)
    eg_block(0)

    def wg(q):
        return remote(wg_parts.at[0], wg_parts.at[q], wg_ssem.at[q], wg_rsem.at[q], ctx=peer_at(q))

    acc = jnp.zeros(routes.shape, f32)
    for i in range(owners):
        expert, _, d = line(i)
        if i:
            remote(wg_send.at[i], wg_recv.at[d], wgz_ssem.at[i], wgz_rsem.at[d], exp=expert).wait_recv()
        acc = acc + jnp.where(routes == expert, wg_recv[d if i else 0, 0:1], 0.0)
    wg_parts[0, 0:routes.shape[0]] = acc
    wg_parts[0, routes.shape[0]:] = jnp.zeros((8 - routes.shape[0], rows), f32)
    for q in others:
        wg(q).start()

    def collect(k, into):
        for i in steps:
            got_result(k, i).wait_recv()
        for n in range(0, columns, step):
            at = slice(n, n + step)
            into[:, at] = jnp.dot(all_picks[...], landing[k, :, at], preferred_element_type=f32).astype(bf)

    collect(0, mixed_ref)
    for q in others:
        wg(q).wait_recv()
        acc = acc + wg_parts[q, 0:routes.shape[0]]
    wgrad_ref[...] = acc
    collect(1, grad_ref)

    for i in steps:
        send_x(i).wait_send()
        rt(i).wait_send()
        wgz(i).wait_send()
        for k in range(2):
            result(k, i).wait_send()
    for q in others:
        wg(q).wait_send()
        for d in range(owners):
            rs(d, q).wait_send()
            bk(d, q).wait_send()
            ag(d, q).wait_send()
            gg(d, q).wait_send()

    @pl.when(z < owners - 1)
    def _():
        far(cot_ref.at[my_half], z, True).wait_send()

    @pl.when(z > 0)
    def _():
        far(cot_ref.at[my_half], z, False).wait_send()

    for d in range(1, owners):
        @pl.when(z - d >= 0)
        def _():
            @pl.when(z < owners - 1)
            def _():
                far(cots.at[z - d, my_half], z - d, True).wait_send()

            sibling(z - d).wait_send()

        @pl.when(z + d < owners)
        def _():
            @pl.when(z > 0)
            def _():
                far(cots.at[z + d, my_half], z + d, False).wait_send()

            sibling(z + d).wait_send()


def hand_over(*refs):
    sems = refs[6]
    copies = [pltpu.make_async_copy(refs[n], refs[n + 3], sems.at[n]) for n in range(3)]
    for copy in copies:
        copy.start()
    for copy in copies:
        copy.wait()


def shards_fused(tokens, routes, event_weights, cotangent, w_gate, w_up, w_down):
    owners, splits = lax.axis_size("exp"), lax.axis_size("ctx")
    _, columns, hidden = w_gate.shape
    rows, fanout = routes.shape
    capacity = max(2, 5 * rows * fanout // (4 * owners))
    part_f = hidden // splits
    sizes = (owners, splits, capacity, rows, columns, hidden)
    bf, f32 = jnp.bfloat16, jnp.float32
    vmem, dma = pltpu.VMEM, pltpu.SemaphoreType.DMA
    full = pl.BlockSpec(memory_space=pltpu.VMEM)
    anywhere = pl.BlockSpec(memory_space=pl.ANY)
    per_block = dma((owners,))
    per_pair = dma((owners, splits))
    moved = owners * capacity * columns
    results = pl.pallas_call(
        functools.partial(fused, sizes),
        out_shape=(
            jax.ShapeDtypeStruct((rows, columns), bf),
            jax.ShapeDtypeStruct((rows, columns), bf),
            jax.ShapeDtypeStruct((fanout, rows), f32),
        ),
        in_specs=[full, full, full, full, anywhere, anywhere, anywhere],
        out_specs=(full, full, full),
        scratch_shapes=[
            vmem((columns, hidden), bf), vmem((columns, hidden), bf), vmem((hidden, columns), bf),
            vmem((owners, capacity, columns), bf), vmem((owners, capacity, columns), bf),
            vmem((owners, 8, rows), f32),
            vmem((owners, rows, columns), bf),
            vmem((owners, splits, 3 * capacity, part_f), bf),
            vmem((owners, splits, 3 * capacity, part_f), bf),
            vmem((owners, splits, capacity, part_f), bf),
            vmem((owners, splits, 2 * capacity, part_f), bf),
            vmem((owners, 2 * capacity, part_f), f32),
            vmem((2, owners, capacity, columns), bf), vmem((2, owners * capacity, columns), bf),
            vmem((rows, owners * capacity), bf),
            vmem((owners, capacity, rows), bf), vmem((owners, capacity, 1), f32),
            vmem((owners, 8, rows), f32), vmem((owners, 8, rows), f32), vmem((splits, 8, rows), f32),
            dma((3,)), per_block, per_block, per_block, per_block,
            per_block, per_block, per_block, per_block, per_block,
            per_pair, per_pair, per_pair, per_pair, per_pair, per_pair, per_pair, per_pair,
            dma((2, owners)), dma((2, owners)), per_block, per_block, dma((splits,)), dma((splits,)),
        ],
        compiler_params=pltpu.CompilerParams(
            collective_id=0, has_side_effects=True, vmem_limit_bytes=56 * 1024 * 1024
        ),
        cost_estimate=pl.CostEstimate(
            flops=12 * moved * hidden, bytes_accessed=6 * columns * hidden, transcendentals=0
        ),
    )(routes.T, event_weights.T, tokens, cotangent, w_gate, w_up, w_down)
    mixed, token_grad, weight_grad = pl.pallas_call(
        hand_over,
        out_shape=tuple(jax.ShapeDtypeStruct(x.shape, x.dtype) for x in results),
        in_specs=[anywhere] * 3,
        out_specs=(anywhere,) * 3,
        scratch_shapes=[dma((3,))],
        cost_estimate=pl.CostEstimate(flops=0, bytes_accessed=8 * rows * columns, transcendentals=0),
    )(*results)
    return mixed, token_grad, weight_grad.T


def fits(mesh, w_gate, routes):
    owners, splits, cores = mesh.shape["exp"], mesh.shape["ctx"], mesh.shape["rep"]
    experts, depth, hidden = w_gate.shape
    rows, fanout = routes.shape[0] // (owners * cores), routes.shape[1]
    capacity = max(2, 5 * rows * fanout // (4 * experts))
    columns = depth // splits
    return (
        experts == owners and owners == 4 and splits > 1 and cores == 2 and fanout == 2
        and rows == 128 and capacity % 16 == 0 and columns % 128 == 0 and hidden % (128 * splits) == 0
        and 6 * columns * hidden <= 16 * 1024 * 1024
    )


def solution(mesh):
    in_specs = (
        P(("rep", "exp"), "ctx"),
        P(("rep", "exp"), None),
        P(("rep", "exp"), None),
        P("exp", "ctx"),
        P("exp", "ctx", None),
        P("exp", "ctx", None),
        P("exp", None, "ctx"),
    )
    out_specs = (P(("rep", "exp"), "ctx"), P(("rep", "exp"), "ctx"), P(("rep", "exp"), None))

    def run(tokens, routes, event_weights, cotangent, w_gate, w_up, w_down):
        body = shards_fused if fits(mesh, w_gate, routes) else shards
        mapped = jax.shard_map(body, mesh=mesh, in_specs=in_specs, out_specs=out_specs, check_vma=False)
        return mapped(tokens, routes, event_weights, cotangent, w_gate, w_up, w_down)

    return run
```
